256 devices in a mesh: img: 8 (over x, core), rows: 32 (over y, z).
Axes of the slice: x: 4, y: 4, z: 8, core: 2. Of those that a mesh axis runs over, the one named last changes fastest.
Arguments:
- feat_fine: bfloat16 [2048, 128, 256], P(('img', 'rows')), parts along dimension 0, may hold values from -6 to 6
- feat_second: bfloat16 [1024, 64, 256], P(('img', 'rows')), parts along dimension 0, may hold values from -6 to 6
- feat_third: bfloat16 [512, 32, 256], P(('img', 'rows')), parts along dimension 0, may hold values from -6 to 6
- conv_weight: bfloat16 [10, 9, 256, 256], replicated, may hold values from -0.125 to 0.125
- conv_bias: float32 [10, 256], replicated, may hold values from -3 to 3
- out_weight: bfloat16 [3, 256, 256], replicated, may hold values from -0.375 to 0.375
- out_bias: float32 [3, 256], replicated, may hold values from -3 to 3
Outputs:
- joined: bfloat16 [4096, 256, 256], P(('img', 'rows')), parts along dimension 0
The draws below stay inside these ranges and needn't reach their ends.
There are 8 independent parts, one for each index of `img`. The reference program is written for one: setup_inputs(seed, part) draws one part's arguments, and reference() takes and returns one part's arrays. A program takes and returns all parts, laid end to end along the dimension named above; an argument that names none is the same for every part. Nothing has to cross between parts.
All inputs are finite; a program needn't handle non-finite values.
Results may differ from the reference program's by a relative error of at most 0.015.
Values may be sent and summed in bfloat16 or wider, within the bound.
No kernel may reach another device: no remote copies, remote signals or barrier semaphores. Data moves between devices by JAX's collectives and lax.ppermute only.
A program may use at most 128 MiB of HBM per device.

```python
import jax
import jax.numpy as jnp
from jax import lax

CH = 256
BASE_COLS = 32
HEIGHT = 64


def steps_of(key, extent, split, least, largest):
    gain = 1.0
    for dim, shards_of in split:
        steps = jax.random.uniform(jax.random.fold_in(jax.random.fold_in(key, 6), dim), (shards_of,), jnp.float32, least / len(split), largest / len(split))
        gain = gain * jnp.repeat(jnp.exp(steps), extent[dim] // shards_of).reshape((-1,) + (1,) * (len(extent) - 1 - dim))
    return gain


def gaussian(own_key, shape, width, limit, pieces=(), kind=jnp.bfloat16):
    values = width * jax.random.normal(own_key, shape, jnp.float32)
    if pieces:
        values = values * steps_of(own_key, shape, pieces, -0.22, 0.18)
    return jnp.clip(values, -limit, limit).astype(kind)


def setup_inputs(seed: int = 0, part: int = 0) -> dict:
    key_list = jax.random.split(jax.random.key(seed), 8)
    own_keys = jax.random.split(jax.random.fold_in(key_list[7], part), 8)
    feat_fine = gaussian(own_keys[0], (4 * HEIGHT, 4 * BASE_COLS, CH), 1.0, 6.0, ((0, 32),))
    feat_second = gaussian(own_keys[1], (2 * HEIGHT, 2 * BASE_COLS, CH), 1.0, 6.0, ((0, 32),))
    feat_third = gaussian(own_keys[2], (HEIGHT, BASE_COLS, CH), 1.0, 6.0, ((0, 32),))
    conv_weight = gaussian(key_list[3], (10, 9, CH, CH), (9 * CH) ** -0.5, 0.125)
    conv_bias = gaussian(key_list[4], (10, CH), 0.5, 3.0, (), jnp.float32)
    out_weight = gaussian(key_list[5], (3, CH, CH), CH ** -0.5, 0.375)
    out_bias = gaussian(key_list[6], (3, CH), 0.5, 3.0, (), jnp.float32)
    return dict(feat_fine=feat_fine, feat_second=feat_second, feat_third=feat_third, conv_weight=conv_weight, conv_bias=conv_bias, out_weight=out_weight, out_bias=out_bias)


def conv_full(source, weight, addend):
    height, columns, channels = source.shape
    padded = jnp.pad(source, ((1, 1), (1, 1), (0, 0)))
    summed = jnp.zeros((height * columns, weight.shape[2]), jnp.float32)
    for offset in range(9):
        window = padded[offset // 3:offset // 3 + height, offset % 3:offset % 3 + columns, :]
        summed = summed + jnp.dot(window.reshape(height * columns, channels), weight[offset], preferred_element_type=jnp.float32)
    return summed.reshape(height, columns, -1) + addend


def residual_unit(source, conv_weight, conv_bias, first):
    hidden = jax.nn.relu(conv_full(jax.nn.relu(source), conv_weight[first], conv_bias[first])).astype(jnp.bfloat16)
    return conv_full(hidden, conv_weight[first + 1], conv_bias[first + 1]) + source.astype(jnp.float32)


def interp_matrix(first_out, count_out, first_in, count_in, size_in):
    outputs = first_out + jnp.arange(count_out, dtype=jnp.int32)
    lowest = (outputs + 1) // 2 - 1
    parity = (outputs % 2).astype(jnp.float32)
    weight_hi = 0.25 + 0.5 * (1.0 - parity)
    low_index = jnp.clip(lowest, 0, size_in - 1).astype(jnp.int32)
    high_index = jnp.clip(lowest + 1, 0, size_in - 1).astype(jnp.int32)
    inputs = first_in + jnp.arange(count_in, dtype=jnp.int32)
    at_low = (inputs[None, :] == low_index[:, None]).astype(jnp.float32)
    at_high = (inputs[None, :] == high_index[:, None]).astype(jnp.float32)
    return (1.0 - weight_hi)[:, None] * at_low + weight_hi[:, None] * at_high


def upsample(source, row_table, col_table):
    rows_in, columns, channels = source.shape
    segmented = jnp.dot(row_table, source.astype(jnp.float32).reshape(rows_in, columns * channels), precision=lax.Precision.HIGHEST)
    segmented = segmented.reshape(-1, columns, channels)
    return jnp.einsum("jw,awc->ajc", col_table, segmented, precision=lax.Precision.HIGHEST).astype(jnp.bfloat16)


def project(lifted, weight, addend):
    flat = lifted.reshape(-1, lifted.shape[2])
    result = jnp.dot(flat, weight, preferred_element_type=jnp.float32) + addend
    return result.astype(jnp.bfloat16).reshape(lifted.shape)


def refine(path, out_weight, out_bias, level):
    rows_in, columns, channels = path.shape
    row_table = interp_matrix(0, 2 * rows_in, 0, rows_in, rows_in)
    col_table = interp_matrix(0, 2 * columns, 0, columns, columns)
    return project(upsample(path, row_table, col_table), out_weight[level], out_bias[level])


def reference(feat_fine, feat_second, feat_third, conv_weight, conv_bias, out_weight, out_bias):
    path = residual_unit(feat_third, conv_weight, conv_bias, 0).astype(jnp.bfloat16)
    path = refine(path, out_weight, out_bias, 0)
    segments = ((feat_second, 2, 1), (feat_fine, 6, 2))
    for feature, first, level in segments:
        merged = (residual_unit(feature, conv_weight, conv_bias, first) + path.astype(jnp.float32)).astype(jnp.bfloat16)
        path = residual_unit(merged, conv_weight, conv_bias, first + 2).astype(jnp.bfloat16)
        path = refine(path, out_weight, out_bias, level)
    return path
```

```python
import functools

import jax
import jax.numpy as jnp
import numpy as np
from jax import lax
from jax.experimental import pallas as pl
from jax.experimental.pallas import tpu as pltpu
from jax.sharding import PartitionSpec as P

CH = 256
TAPS = 9 * CH
BF = jnp.bfloat16
F32 = jnp.float32
VMEM_LIMIT = 56 * 1024 * 1024


def pair_table(columns):
    cols = np.zeros((2 * columns, columns), np.float32)
    for m in range(columns):
        cols[2 * m, max(m - 1, 0)] += 0.25
        cols[2 * m, m] += 0.75
        cols[2 * m + 1, m] += 0.75
        cols[2 * m + 1, min(m + 1, columns - 1)] += 0.25
    table = np.block([[0.75 * cols, 0.25 * cols], [0.25 * cols, 0.75 * cols]])
    return jnp.asarray(table, BF)


def store_taps(dst, row, value, columns):
    cells = value.shape[0]
    rows = cells // columns
    column = lax.broadcasted_iota(jnp.int32, (cells, 1), 0) % columns
    left = jnp.where(column == 0, 0.0, pltpu.roll(value, 1, 0))
    right = jnp.where(column == columns - 1, 0.0, pltpu.roll(value, cells - 1, 0))
    for part, piece in enumerate((left, value, right)):
        dst[pl.ds(row, rows), :, part * CH : (part + 1) * CH] = piece.astype(BF).reshape(
            rows, columns, CH
        )


def conv(src, row, rows, columns, weight, bias):
    lhs = jnp.concatenate(
        [src[pl.ds(row + a, rows)].reshape(rows * columns, 3 * CH) for a in range(3)], axis=1
    )
    return jnp.dot(lhs, weight, preferred_element_type=F32) + bias


def inside(value, first, columns, height):
    cells = value.shape[0]
    row = first + lax.broadcasted_iota(jnp.int32, (cells, 1), 0) // columns
    return jnp.where((row >= 0) & (row < height), value, 0.0)


def chunks(rows, step):
    return [(r, min(step, rows - r)) for r in range(0, rows, step)]


class Weights:
    def __init__(self, hbm, vmem, sems, first):
        self.vmem = vmem
        self.copies = [
            pltpu.make_async_copy(hbm.at[first + k], vmem.at[k], sems.at[k])
            for k in range(vmem.shape[0])
        ]
        for copy in self.copies:
            copy.start()

    def wait(self, k):
        self.copies[k].wait()
        return self.vmem[k]


def clamp_edges(v, above, first_row, below, last_row, position, ends):
    @pl.when(position == 0)
    def _():
        v[above] = v[first_row]

    @pl.when(position == ends)
    def _():
        v[below] = v[last_row]


def coarse_kernel(
    third, second, m1, p1, m2, p2, table3, conv_bias, out_weight, out_bias, conv_weight,
    ref_out, w, sems, x3, h3, v3, x2, h2, p2nd, merged,
):
    position = lax.axis_index("rows")
    ends = lax.axis_size("rows") - 1
    weights = Weights(conv_weight, w, sems, 0)

    c3 = 32
    raw3 = jnp.concatenate(
        [m2[...], m1[0:64], third[...].reshape(64, CH), p1[0:64], p2[...]], axis=0
    ).astype(F32)
    base3 = 2 * position
    h_third = 2 * (ends + 1)
    store_taps(x3, 0, inside(jnp.maximum(raw3, 0.0), base3 - 4, c3, h_third), c3)
    c2 = 64
    base2 = 4 * position
    h_second = 4 * (ends + 1)
    raw2 = (m1[64:320], second[...].reshape(256, CH), p1[64:320])
    for part in range(3):
        value = jnp.maximum(raw2[part].astype(F32), 0.0)
        store_taps(x2, 4 * part, inside(value, base2 + 4 * part - 4, c2, h_second), c2)

    hid = jnp.maximum(conv(x3, 0, 8, c3, weights.wait(0), conv_bias[0:1]), 0.0)
    store_taps(h3, 0, inside(hid, base3 - 3, c3, h_third), c3)
    path = conv(h3, 0, 6, c3, weights.wait(1), conv_bias[1:2]) + raw3[64:256]
    v3[...] = path.astype(BF).reshape(6, c3, CH)
    clamp_edges(v3, 1, 2, 4, 3, position, ends)
    u = (
        jnp.dot(v3[...].reshape(6 * c3, CH), out_weight[0], preferred_element_type=F32)
        + out_bias[0:1]
    ).astype(BF)
    for j in range(5):
        two = jnp.dot(
            table3[...], u[j * c3 : (j + 2) * c3], preferred_element_type=F32
        ).astype(BF)
        if j > 0:
            p2nd[2 * j - 1] = two[0:c2]
        if j < 4:
            p2nd[2 * j] = two[c2 : 2 * c2]

    wk = weights.wait(2)
    for r, n in chunks(10, 5):
        hid = jnp.maximum(conv(x2, r, n, c2, wk, conv_bias[2:3]), 0.0)
        store_taps(h2, r, inside(hid, base2 - 3 + r, c2, h_second), c2)
    wk = weights.wait(3)
    for r, n in chunks(8, 2):
        lateral = conv(h2, r, n, c2, wk, conv_bias[3:4])
        part = raw2[(r + 2) // 4]
        at = (r + 2) % 4
        lateral = lateral + part[at * c2 : (at + n) * c2].astype(F32)
        joined = (lateral + p2nd[pl.ds(r, n)].reshape(n * c2, CH).astype(F32)).astype(BF)
        merged[pl.ds(r, n)] = joined.reshape(n, c2, CH)
        value = jnp.maximum(joined.astype(F32), 0.0)
        store_taps(x2, r, inside(value, base2 - 2 + r, c2, h_second), c2)
    wk = weights.wait(4)
    for r, n in chunks(6, 6):
        hid = jnp.maximum(conv(x2, r, n, c2, wk, conv_bias[4:5]), 0.0)
        store_taps(h2, r, inside(hid, base2 - 1 + r, c2, h_second), c2)
    wk = weights.wait(5)
    for r, n in chunks(4, 4):
        refined = conv(h2, r, n, c2, wk, conv_bias[5:6])
        refined = refined + merged[pl.ds(r + 2, n)].reshape(n * c2, CH).astype(F32)
        ref_out[pl.ds(r, n)] = refined.astype(BF).reshape(n, c2, CH)


def fine_hidden_kernel(
    fine, mf, pf, conv_bias, conv_weight, hid_out, w, sems, x1,
):
    position = lax.axis_index("rows")
    ends = lax.axis_size("rows") - 1
    weights = Weights(conv_weight, w, sems, 6)
    c1 = 128
    base = 8 * position
    height = 8 * (ends + 1)
    row = 0
    for ref, rows in ((mf, 5), (fine, 8), (pf, 5)):
        for r, n in chunks(rows, 4):
            value = jnp.maximum(ref[pl.ds(r, n)].reshape(n * c1, CH).astype(F32), 0.0)
            store_taps(x1, row + r, inside(value, base + row + r - 5, c1, height), c1)
        row += rows
    wk = weights.wait(0)
    for r, n in chunks(16, 4):
        hid = jnp.maximum(conv(x1, r, n, c1, wk, conv_bias[6:7]), 0.0)
        hid = inside(hid, base - 4 + r, c1, height).astype(BF)
        hid_out[pl.ds(r, n)] = hid.reshape(n, c1, CH)


def fine_kernel(
    fine, mf, pf, hid_in, ref, mr, pr, table2, table1, conv_bias, out_weight, out_bias,
    conv_weight, out, w, sems, h1, x1, v2, p1st, merged, v1, u1,
):
    position = lax.axis_index("rows")
    ends = lax.axis_size("rows") - 1
    weights = Weights(conv_weight, w, sems, 7)
    c2, c1 = 64, 128
    base = 8 * position
    height = 8 * (ends + 1)

    for r, n in chunks(16, 4):
        store_taps(h1, r, hid_in[pl.ds(r, n)].reshape(n * c1, CH).astype(F32), c1)

    v2[0:2] = mr[...]
    v2[2:6] = ref[...]
    v2[6:8] = pr[...]
    clamp_edges(v2, 1, 2, 6, 5, position, ends)
    u = (
        jnp.dot(v2[...].reshape(8 * c2, CH), out_weight[1], preferred_element_type=F32)
        + out_bias[1:2]
    ).astype(BF)
    for j in range(7):
        two = jnp.dot(
            table2[...], u[j * c2 : (j + 2) * c2], preferred_element_type=F32
        ).astype(BF)
        p1st[2 * j : 2 * j + 2] = two.reshape(2, c1, CH)

    wk = weights.wait(0)
    for r, n in ((0, 2), (2, 4), (6, 4), (10, 1), (11, 3)):
        lateral = conv(h1, r, n, c1, wk, conv_bias[7:8])
        if r < 2:
            source = mf[pl.ds(r + 2, n)]
        elif r == 10:
            source = fine[pl.ds(r - 3, n)]
        elif r < 10:
            source = jnp.concatenate([mf[4:5], fine[0:3]], axis=0) if r == 2 else fine[3:7]
        else:
            source = pf[pl.ds(r - 11, n)]
        lateral = lateral + source.reshape(n * c1, CH).astype(F32)
        joined = (lateral + p1st[pl.ds(r, n)].reshape(n * c1, CH).astype(F32)).astype(BF)
        merged[pl.ds(r, n)] = joined.reshape(n, c1, CH)
        value = jnp.maximum(joined.astype(F32), 0.0)
        store_taps(x1, r, inside(value, base - 3 + r, c1, height), c1)
    wk = weights.wait(1)
    for r, n in chunks(12, 4):
        hid = jnp.maximum(conv(x1, r, n, c1, wk, conv_bias[8:9]), 0.0)
        store_taps(h1, r, inside(hid, base - 2 + r, c1, height), c1)
    wk = weights.wait(2)
    for r, n in chunks(10, 5):
        refined = conv(h1, r, n, c1, wk, conv_bias[9:10])
        refined = refined + merged[pl.ds(r + 2, n)].reshape(n * c1, CH).astype(F32)
        v1[pl.ds(r, n)] = refined.astype(BF).reshape(n, c1, CH)
    clamp_edges(v1, 0, 1, 9, 8, position, ends)
    for r, n in chunks(10, 5):
        u1[r * c1 : (r + n) * c1] = (
            jnp.dot(v1[pl.ds(r, n)].reshape(n * c1, CH), out_weight[2], preferred_element_type=F32)
            + out_bias[2:3]
        ).astype(BF)
    for j in range(9):
        src = u1[j * c1 : (j + 2) * c1]
        if j == 0:
            out[0] = jnp.dot(table1[2 * c1 :], src, preferred_element_type=F32).astype(BF)
        elif j == 8:
            out[15] = jnp.dot(table1[0 : 2 * c1], src, preferred_element_type=F32).astype(BF)
        else:
            two = jnp.dot(table1[...], src, preferred_element_type=F32).astype(BF)
            out[2 * j - 1 : 2 * j + 1] = two.reshape(2, 2 * c1, CH)


VM = pl.BlockSpec(memory_space=pltpu.VMEM)
ANY = pl.BlockSpec(memory_space=pl.ANY)


def call(kernel, args, in_specs, out_shape, scratch, flops):
    return pl.pallas_call(
        kernel,
        out_shape=jax.ShapeDtypeStruct(out_shape, BF),
        in_specs=in_specs,
        out_specs=VM,
        scratch_shapes=scratch,
        compiler_params=pltpu.CompilerParams(vmem_limit_bytes=VMEM_LIMIT),
        cost_estimate=pl.CostEstimate(flops=flops, bytes_accessed=4_000_000, transcendentals=0),
    )(*args)


def weight_scratch(count):
    return [pltpu.VMEM((count, TAPS, CH), BF), pltpu.SemaphoreType.DMA((count,))]


def local(feat_fine, feat_second, feat_third, conv_weight, conv_bias, out_weight, out_bias):
    devices = lax.axis_size("rows")

    def shift(value, step):
        return lax.ppermute(value, "rows", [(i, (i + step) % devices) for i in range(devices)])

    weight = conv_weight.reshape(10, TAPS, CH)
    third = feat_third.reshape(64, CH)
    pack = jnp.concatenate([third, feat_second.reshape(256, CH)], axis=0)
    m1, p1 = shift(pack, 1), shift(pack, -1)
    m2, p2 = shift(third, 2), shift(third, -2)
    mf, pf = shift(feat_fine[3:8], 1), shift(feat_fine[0:5], -1)

    ref = call(
        coarse_kernel,
        (feat_third, feat_second, m1, p1, m2, p2, pair_table(32), conv_bias, out_weight, out_bias, weight),
        [VM] * 10 + [ANY],
        (4, 64, CH),
        weight_scratch(6)
        + [
            pltpu.VMEM((10, 32, 3 * CH), BF),
            pltpu.VMEM((8, 32, 3 * CH), BF),
            pltpu.VMEM((6, 32, CH), BF),
            pltpu.VMEM((12, 64, 3 * CH), BF),
            pltpu.VMEM((10, 64, 3 * CH), BF),
            pltpu.VMEM((8, 64, CH), BF),
            pltpu.VMEM((8, 64, CH), BF),
        ],
        2_000_000_000,
    )
    mr, pr = shift(ref[2:4], 1), shift(ref[0:2], -1)
    hid = call(
        fine_hidden_kernel,
        (feat_fine, mf, pf, conv_bias, weight),
        [VM] * 4 + [ANY],
        (16, 128, CH),
        weight_scratch(1) + [pltpu.VMEM((18, 128, 3 * CH), BF)],
        2_400_000_000,
    )
    return call(
        fine_kernel,
        (feat_fine, mf, pf, hid, ref, mr, pr, pair_table(64), pair_table(128), conv_bias, out_weight, out_bias, weight),
        [VM] * 12 + [ANY],
        (16, 256, CH),
        weight_scratch(3)
        + [
            pltpu.VMEM((16, 128, 3 * CH), BF),
            pltpu.VMEM((14, 128, 3 * CH), BF),
            pltpu.VMEM((8, 64, CH), BF),
            pltpu.VMEM((14, 128, CH), BF),
            pltpu.VMEM((14, 128, CH), BF),
            pltpu.VMEM((10, 128, CH), BF),
            pltpu.VMEM((1280, CH), BF),
        ],
        6_000_000_000,
    )


def solution(mesh):
    rows = P(("img", "rows"), None, None)
    return jax.shard_map(
        local,
        mesh=mesh,
        in_specs=(rows, rows, rows, P(), P(), P(), P()),
        out_specs=rows,
        check_vma=False,
    )
```

```python
import functools

import jax
import jax.numpy as jnp
import numpy as np
from jax import lax
from jax.experimental import pallas as pl
from jax.experimental.pallas import tpu as pltpu
from jax.sharding import PartitionSpec as P

CH = 256
TAPS = 9 * CH
BF = jnp.bfloat16
F32 = jnp.float32
VMEM_LIMIT = 28 * 1024 * 1024


def pair_table(columns):
    cols = np.zeros((2 * columns, columns), np.float32)
    for m in range(columns):
        cols[2 * m, max(m - 1, 0)] += 0.25
        cols[2 * m, m] += 0.75
        cols[2 * m + 1, m] += 0.75
        cols[2 * m + 1, min(m + 1, columns - 1)] += 0.25
    table = np.block([[0.75 * cols, 0.25 * cols], [0.25 * cols, 0.75 * cols]])
    return jnp.asarray(table, BF)


def store_taps(dst, row, value, columns):
    cells = value.shape[0]
    rows = cells // columns
    column = lax.broadcasted_iota(jnp.int32, (cells, 1), 0) % columns
    left = jnp.where(column == 0, 0.0, pltpu.roll(value, 1, 0))
    right = jnp.where(column == columns - 1, 0.0, pltpu.roll(value, cells - 1, 0))
    for part, piece in enumerate((left, value, right)):
        dst[pl.ds(row, rows), :, part * CH : (part + 1) * CH] = piece.astype(BF).reshape(
            rows, columns, CH
        )


def conv(src, row, rows, columns, weight, bias):
    lhs = jnp.concatenate(
        [src[pl.ds(row + a, rows)].reshape(rows * columns, 3 * CH) for a in range(3)], axis=1
    )
    return jnp.dot(lhs, weight, preferred_element_type=F32) + bias


def inside(value, first, columns, height):
    cells = value.shape[0]
    row = first + lax.broadcasted_iota(jnp.int32, (cells, 1), 0) // columns
    return jnp.where((row >= 0) & (row < height), value, 0.0)


def chunks(rows, step):
    return [(r, min(step, rows - r)) for r in range(0, rows, step)]


def clamp_edges(v, above, first_row, below, last_row, position, ends):
    @pl.when(position == 0)
    def _():
        v[above] = v[first_row]

    @pl.when(position == ends)
    def _():
        v[below] = v[last_row]


def project(cells, weight, bias):
    return (jnp.dot(cells, weight, preferred_element_type=F32) + bias).astype(BF)


def lift(table, cells):
    return jnp.dot(table, cells, preferred_element_type=F32).astype(BF)


def load(sems, *pairs):
    copies = [pltpu.make_async_copy(src, dst, sems.at[k]) for k, (src, dst) in enumerate(pairs)]
    for copy in copies:
        copy.start()
    return copies


def pair_up(hop, devices, parts):
    inner = [i ^ hop for i in range(devices)]
    outer = [((i - hop) ^ hop) + hop for i in range(devices)]
    return [
        [
            (p * devices + i, p * devices + j if 0 <= j < devices else (p ^ 1) * devices + i)
            for p in range(parts)
            for i, j in enumerate(ends)
        ]
        for ends in (inner, outer)
    ]


def first_half(hop):
    return (lax.axis_index("rows") // hop) % 2 == 0


def sides(inner, outer, hop):
    lower = first_half(hop)
    return jnp.where(lower, outer, inner), jnp.where(lower, inner, outer)


def pack_kernel(third, second, fine, pack, inner, outer, sems):
    lower = first_half(1)
    start = [pl.multiple_of(jnp.where(lower == flag, 384, 0), 128) for flag in (True, False)]
    copies = load(
        sems,
        (fine.at[pl.ds(start[0], 640)], inner),
        (fine.at[pl.ds(start[1], 640)], outer),
        (second, pack.at[pl.ds(64, 256)]),
        (third, pack.at[pl.ds(0, 64)]),
    )
    for copy in copies:
        copy.wait()


def coarse_kernel(
    inner1, outer1, inner2, outer2, third_any, second_any, table_any, conv_weight, bias_any, ow_any, ob_any,
    ref_inner, ref_outer, third, second, table3, w, conv_bias, out_weight, out_bias, x3, h3, v3, x2,
    h2, p2nd, merged, refs, sems,
):
    copies = load(
        sems,
        (third_any, third),
        (second_any, second),
        (bias_any, conv_bias),
        (conv_weight.at[0], w.at[0]),
        (conv_weight.at[1], w.at[1]),
        (ow_any.at[0], out_weight),
        (ob_any, out_bias),
        (table_any, table3),
        *((conv_weight.at[k], w.at[k]) for k in range(2, 6)),
    )
    position = lax.axis_index("rows")
    ends = lax.axis_size("rows") - 1
    c3, c2 = 32, 64
    base3, base2 = 2 * position, 4 * position
    high3, high2 = 2 * (ends + 1), 4 * (ends + 1)

    m1, p1 = sides(inner1[...], outer1[...], 1)
    m2, p2 = sides(inner2[...], outer2[...], 2)
    for row, part in ((0, m1), (8, p1)):
        value = jnp.maximum(part[64:320].astype(F32), 0.0)
        store_taps(x2, row, inside(value, base2 + row - 4, c2, high2), c2)
    copies[0].wait()
    raw3 = jnp.concatenate([m2, m1[0:64], third[...], p1[0:64], p2], axis=0).astype(F32)
    store_taps(x3, 0, inside(jnp.maximum(raw3, 0.0), base3 - 4, c3, high3), c3)
    copies[1].wait()
    store_taps(x2, 4, jnp.maximum(second[...].astype(F32), 0.0), c2)
    copies[2].wait()
    copies[3].wait()
    hid = jnp.maximum(conv(x3, 0, 8, c3, w[0], conv_bias[0:1]), 0.0)
    store_taps(h3, 0, inside(hid, base3 - 3, c3, high3), c3)
    copies[4].wait()
    path = conv(h3, 0, 6, c3, w[1], conv_bias[1:2]) + raw3[64:256]
    v3[...] = path.astype(BF).reshape(6, c3, CH)
    clamp_edges(v3, 1, 2, 4, 3, position, ends)
    for copy in copies[5:9]:
        copy.wait()
    u = project(v3[...].reshape(6 * c3, CH), out_weight[...], out_bias[0:1])
    for j in range(5):
        two = lift(table3[...], u[j * c3 : (j + 2) * c3])
        if j > 0:
            p2nd[2 * j - 1] = two[0:c2]
        if j < 4:
            p2nd[2 * j] = two[c2 : 2 * c2]

    for r, n in chunks(10, 5):
        hid = jnp.maximum(conv(x2, r, n, c2, w[2], conv_bias[2:3]), 0.0)
        store_taps(h2, r, inside(hid, base2 - 3 + r, c2, high2), c2)
    copies[9].wait()
    raw2 = jnp.concatenate([m1[192:320], second[...], p1[64:192]], axis=0)
    for r, n in chunks(8, 4):
        lateral = conv(h2, r, n, c2, w[3], conv_bias[3:4])
        lateral = lateral + raw2[r * c2 : (r + n) * c2].astype(F32)
        joined = (lateral + p2nd[pl.ds(r, n)].reshape(n * c2, CH).astype(F32)).astype(BF)
        merged[pl.ds(r, n)] = joined.reshape(n, c2, CH)
        value = jnp.maximum(joined.astype(F32), 0.0)
        store_taps(x2, r, inside(value, base2 - 2 + r, c2, high2), c2)
    copies[10].wait()
    for r, n in chunks(6, 6):
        hid = jnp.maximum(conv(x2, r, n, c2, w[4], conv_bias[4:5]), 0.0)
        store_taps(h2, r, inside(hid, base2 - 1 + r, c2, high2), c2)
    copies[11].wait()
    refined = conv(h2, 0, 4, c2, w[5], conv_bias[5:6])
    refined = refined + merged[2:6].reshape(4 * c2, CH).astype(F32)
    refs[...] = refined.astype(BF).reshape(4, c2, CH)
    lower = first_half(1)
    ref_inner[...] = refs[pl.ds(jnp.where(lower, 2, 0), 2)]
    ref_outer[...] = refs[pl.ds(jnp.where(lower, 0, 2), 2)]


def fine_hidden_kernel(
    inner, outer, fine_any, conv_weight, bias_any, h1, fine, w, conv_bias, x1, sems,
):
    copies = load(
        sems, (fine_any, fine), (conv_weight.at[6], w), (bias_any, conv_bias)
    )
    position = lax.axis_index("rows")
    ends = lax.axis_size("rows") - 1
    c1 = 128
    base = 8 * position
    height = 8 * (ends + 1)
    for row, part in zip((0, 13), sides(inner[...], outer[...], 1)):
        value = jnp.maximum(part.astype(F32), 0.0)
        store_taps(x1, row, inside(value, base + row - 5, c1, height), c1)
    copies[0].wait()
    for r in (0, 4):
        store_taps(x1, 5 + r, jnp.maximum(fine[r * c1 : (r + 4) * c1].astype(F32), 0.0), c1)
    copies[1].wait()
    copies[2].wait()
    for r, n in chunks(16, 4):
        hid = jnp.maximum(conv(x1, r, n, c1, w[...], conv_bias[6:7]), 0.0)
        store_taps(h1, r, inside(hid, base - 4 + r, c1, height), c1)


def fine_kernel(
    inner, outer, h1, ref_inner, ref_outer, inner_r, outer_r, fine_any, conv_weight, bias_any, ow_any, ob_any,
    table2_any, table1_any, out, fine, w, conv_bias, out_weight, out_bias, table2, table1, v2,
    p1st, x1, hb, merged, v1, u1, staged, sems,
):
    copies = load(
        sems,
        (ow_any, out_weight),
        (ob_any, out_bias),
        (table2_any, table2),
        (conv_weight.at[7], w.at[0]),
        (bias_any, conv_bias),
        (fine_any, fine),
        (conv_weight.at[8], w.at[1]),
        (conv_weight.at[9], w.at[2]),
        (table1_any, table1),
    )
    position = lax.axis_index("rows")
    ends = lax.axis_size("rows") - 1
    c2, c1 = 64, 128
    base = 8 * position
    height = 8 * (ends + 1)

    mf, pf = sides(inner[...], outer[...], 1)
    v2[0:2], v2[6:8] = sides(inner_r[...], outer_r[...], 1)
    v2[2:4], v2[4:6] = sides(ref_outer[...], ref_inner[...], 1)[::-1]
    clamp_edges(v2, 1, 2, 6, 5, position, ends)
    for copy in copies[0:3]:
        copy.wait()
    u = project(v2[...].reshape(8 * c2, CH), out_weight[1], out_bias[1:2])
    for j in range(7):
        two = lift(table2[...], u[j * c2 : (j + 2) * c2])
        p1st[2 * j : 2 * j + 2] = two.reshape(2, c1, CH)
    for copy in copies[3:6]:
        copy.wait()
    raw = jnp.concatenate([mf[256:640], fine[...], pf[0:384]], axis=0)
    for r, n in chunks(14, 4):
        lateral = conv(h1, r, n, c1, w[0], conv_bias[7:8])
        lateral = lateral + raw[r * c1 : (r + n) * c1].astype(F32)
        joined = (lateral + p1st[pl.ds(r, n)].reshape(n * c1, CH).astype(F32)).astype(BF)
        merged[pl.ds(r, n)] = joined.reshape(n, c1, CH)
        value = jnp.maximum(joined.astype(F32), 0.0)
        store_taps(x1, r, inside(value, base - 3 + r, c1, height), c1)
    copies[6].wait()
    for r, n in chunks(12, 4):
        hid = jnp.maximum(conv(x1, r, n, c1, w[1], conv_bias[8:9]), 0.0)
        store_taps(hb, r, inside(hid, base - 2 + r, c1, height), c1)
    copies[7].wait()
    for r, n in chunks(10, 5):
        refined = conv(hb, r, n, c1, w[2], conv_bias[9:10])
        refined = refined + merged[pl.ds(r + 2, n)].reshape(n * c1, CH).astype(F32)
        v1[pl.ds(r, n)] = refined.astype(BF).reshape(n, c1, CH)
    clamp_edges(v1, 0, 1, 9, 8, position, ends)
    copies[8].wait()
    for r, n in chunks(10, 5):
        u1[r * c1 : (r + n) * c1] = project(
            v1[pl.ds(r, n)].reshape(n * c1, CH), out_weight[2], out_bias[2:3]
        )
    copies = []
    for j in range(9):
        first, count = max(2 * j - 1, 0), 2 if 0 < j < 8 else 1
        half = slice(2 * c1 if j == 0 else 0, 2 * c1 if j == 8 else 4 * c1)
        rows = lift(table1[half], u1[j * c1 : (j + 2) * c1])
        staged[pl.ds(first, count)] = rows.reshape(count, 2 * c1, CH)
        copies.append(
            pltpu.make_async_copy(
                staged.at[pl.ds(first, count)], out.at[pl.ds(first, count)], sems.at[j]
            )
        )
        copies[-1].start()
    for copy in copies:
        copy.wait()


VM = pl.BlockSpec(memory_space=pltpu.VMEM)
ANY = pl.BlockSpec(memory_space=pltpu.HBM)


def call(kernel, in_vmem, in_hbm, shapes, out_spec, scratch, sems, flops):
    outs = [jax.ShapeDtypeStruct(shape, BF) for shape in shapes]
    return pl.pallas_call(
        kernel,
        out_shape=outs,
        in_specs=[VM] * len(in_vmem) + [ANY] * len(in_hbm),
        out_specs=[out_spec] * len(outs),
        scratch_shapes=[pltpu.VMEM(shape, kind) for shape, kind in scratch]
        + [pltpu.SemaphoreType.DMA((sems,))],
        compiler_params=pltpu.CompilerParams(vmem_limit_bytes=VMEM_LIMIT),
        cost_estimate=pl.CostEstimate(flops=flops, bytes_accessed=1_000_000, transcendentals=0),
    )(*in_vmem, *(pltpu.with_memory_space_constraint(x, pltpu.HBM) for x in in_hbm))


def local(feat_fine, feat_second, feat_third, conv_weight, conv_bias, out_weight, out_bias):
    devices = lax.axis_size("rows")

    def exchange(value_in, value_out, hop):
        values = (value_in, value_out)
        pairs = pair_up(hop, devices, lax.axis_size("img"))
        return [lax.ppermute(v, ("img", "rows"), p) for v, p in zip(values, pairs)]

    weight = conv_weight.reshape(10, TAPS, CH)
    third = feat_third.reshape(64, CH)
    second = feat_second.reshape(256, CH)
    fine = feat_fine.reshape(1024, CH)
    pack, fine_in, fine_out = call(
        pack_kernel, (), (third, second, fine), ((320, CH), (640, CH), (640, CH)), VM, [], 4, 1000
    )
    near = exchange(pack, pack, 1)
    far = exchange(third, third, 2)
    halo = exchange(fine_in, fine_out, 1)
    refs = call(
        coarse_kernel,
        (*near, *far),
        (third, second, pair_table(32), weight, conv_bias, out_weight, out_bias),
        ((2, 64, CH), (2, 64, CH)),
        VM,
        [
            ((64, CH), BF),
            ((256, CH), BF),
            ((128, 64), BF),
            ((6, TAPS, CH), BF),
            ((10, CH), F32),
            ((CH, CH), BF),
            ((3, CH), F32),
            ((10, 32, 3 * CH), BF),
            ((8, 32, 3 * CH), BF),
            ((6, 32, CH), BF),
            ((12, 64, 3 * CH), BF),
            ((10, 64, 3 * CH), BF),
            ((8, 64, CH), BF),
            ((8, 64, CH), BF),
            ((4, 64, CH), BF),
        ],
        12,
        40_000_000_000,
    )
    got = exchange(*refs, 1)
    (h1,) = call(
        fine_hidden_kernel,
        (*halo,),
        (fine, weight, conv_bias),
        ((16, 128, 3 * CH),),
        VM,
        [
            ((1024, CH), BF),
            ((TAPS, CH), BF),
            ((10, CH), F32),
            ((18, 128, 3 * CH), BF),
        ],
        3,
        2_400_000_000,
    )
    (out,) = call(
        fine_kernel,
        (*halo, h1, *refs, *got),
        (fine, weight, conv_bias, out_weight, out_bias, pair_table(64), pair_table(128)),
        ((16, 256, CH),),
        ANY,
        [
            ((1024, CH), BF),
            ((3, TAPS, CH), BF),
            ((10, CH), F32),
            ((3, CH, CH), BF),
            ((3, CH), F32),
            ((256, 128), BF),
            ((512, 256), BF),
            ((8, 64, CH), BF),
            ((14, 128, CH), BF),
            ((14, 128, 3 * CH), BF),
            ((12, 128, 3 * CH), BF),
            ((14, 128, CH), BF),
            ((10, 128, CH), BF),
            ((1280, CH), BF),
            ((16, 256, CH), BF),
        ],
        9,
        6_000_000_000,
    )
    return out


def solution(mesh):
    rows = P(("img", "rows"), None, None)
    return jax.shard_map(
        local,
        mesh=mesh,
        in_specs=(rows, rows, rows, P(), P(), P(), P()),
        out_specs=rows,
        check_vma=False,
    )
```

```python
import functools

import jax
import jax.numpy as jnp
import numpy as np
from jax import lax
from jax.experimental import pallas as pl
from jax.experimental.pallas import tpu as pltpu
from jax.sharding import PartitionSpec as P

CH = 256
TAPS = 9 * CH
BF = jnp.bfloat16
F32 = jnp.float32
FETCH_COST = 2_000_000_000
PACK_COST = 20_000_000_000
VMEM_LIMIT = 20 * 1024 * 1024


def pair_table(columns):
    cols = np.zeros((2 * columns, columns), np.float32)
    for m in range(columns):
        cols[2 * m, max(m - 1, 0)] += 0.25
        cols[2 * m, m] += 0.75
        cols[2 * m + 1, m] += 0.75
        cols[2 * m + 1, min(m + 1, columns - 1)] += 0.25
    table = np.block([[0.75 * cols, 0.25 * cols], [0.25 * cols, 0.75 * cols]])
    return jnp.asarray(table, BF)


def store_taps(dst, row, value, columns):
    cells = value.shape[0]
    rows = cells // columns
    column = lax.broadcasted_iota(jnp.int32, (cells, 1), 0) % columns
    left = jnp.where(column == 0, 0.0, pltpu.roll(value, 1, 0))
    right = jnp.where(column == columns - 1, 0.0, pltpu.roll(value, cells - 1, 0))
    for part, piece in enumerate((left, value, right)):
        dst[pl.ds(row, rows), :, part * CH : (part + 1) * CH] = piece.astype(BF).reshape(
            rows, columns, CH
        )


def conv(src, row, rows, columns, weight, bias):
    lhs = jnp.concatenate(
        [src[pl.ds(row + a, rows)].reshape(rows * columns, 3 * CH) for a in range(3)], axis=1
    )
    return jnp.dot(lhs, weight, preferred_element_type=F32) + bias


def inside(value, first, columns, height):
    cells = value.shape[0]
    row = first + lax.broadcasted_iota(jnp.int32, (cells, 1), 0) // columns
    return jnp.where((row >= 0) & (row < height), value, 0.0)


def chunks(rows, step):
    return [(r, min(step, rows - r)) for r in range(0, rows, step)]


def project(cells, weight, bias):
    return (jnp.dot(cells, weight, preferred_element_type=F32) + bias).astype(BF)


def lift(table, cells):
    return jnp.dot(table, cells, preferred_element_type=F32).astype(BF)


def load(sems, *pairs):
    copies = [pltpu.make_async_copy(src, dst, sems.at[k]) for k, (src, dst) in enumerate(pairs)]
    for copy in copies:
        copy.start()
    return copies


def pair_up(hop, devices, parts):
    inner = [i ^ hop for i in range(devices)]
    outer = [((i - hop) ^ hop) + hop for i in range(devices)]
    return [
        [
            (p * devices + i, p * devices + j if 0 <= j < devices else (p ^ 1) * devices + i)
            for p in range(parts)
            for i, j in enumerate(ends)
        ]
        for ends in (inner, outer)
    ]


def first_half(hop):
    return (lax.axis_index("rows") // hop) % 2 == 0


def sides(inner, outer, hop):
    lower = first_half(hop)
    return jnp.where(lower, outer, inner), jnp.where(lower, inner, outer)


def edge_rows(fine, flag):
    start = jnp.where(first_half(1) == flag, 384, 0)
    return fine.at[pl.ds(pl.multiple_of(start, 128), 640)]


def pack_kernel(third, second, fine, pack, inner, outer, sems):
    copies = load(
        sems,
        (edge_rows(fine, True), inner),
        (edge_rows(fine, False), outer),
        (second, pack.at[pl.ds(64, 256)]),
        (third, pack.at[pl.ds(0, 64)]),
    )
    for copy in copies:
        copy.wait()


def middle_kernel(fine, w, conv_bias, h_mid, lat_mid, x1):
    c1 = 128
    for r in (0, 4):
        store_taps(x1, r, jnp.maximum(fine[r * c1 : (r + 4) * c1].astype(F32), 0.0), c1)
    for r, n in chunks(6, 3):
        hid = jnp.maximum(conv(x1, r, n, c1, w[6], conv_bias[6:7]), 0.0)
        store_taps(h_mid, r, hid, c1)
    lat_mid[...] = conv(h_mid, 0, 4, c1, w[7], conv_bias[7:8]) + fine[2 * c1 : 6 * c1].astype(F32)


def clamped(above, own, below, columns):
    position = lax.axis_index("rows")
    ends = lax.axis_size("rows") - 1
    last = above.shape[0] - columns
    above_row = jnp.where(position == 0, own[0:columns], above[last:])
    below_row = jnp.where(position == ends, own[own.shape[0] - columns :], below[0:columns])
    return jnp.concatenate([above[0:last], above_row, own, below_row, below[columns:]], axis=0)


def coarse_kernel(
    inner1, outer1, inner2, outer2, second, third, w, conv_bias, out_weight, out_bias, table3,
    u_inner, u_outer, x3, h3, x2, h2, p2nd, merged, kept,
):
    position = lax.axis_index("rows")
    ends = lax.axis_size("rows") - 1
    c3, c2 = 32, 64
    base3, base2 = 2 * position, 4 * position
    high3, high2 = 2 * (ends + 1), 4 * (ends + 1)
    m1, p1 = sides(inner1[...], outer1[...], 1)
    m2, p2 = sides(inner2[...], outer2[...], 2)

    raw3 = jnp.concatenate([m2, m1[0:64], third[...], p1[0:64], p2], axis=0).astype(F32)
    store_taps(x3, 0, inside(jnp.maximum(raw3, 0.0), base3 - 4, c3, high3), c3)
    for row, part in ((0, m1[64:320]), (4, second[...]), (8, p1[64:320])):
        value = jnp.maximum(part.astype(F32), 0.0)
        store_taps(x2, row, inside(value, base2 + row - 4, c2, high2), c2)

    hid = jnp.maximum(conv(x3, 0, 8, c3, w[0], conv_bias[0:1]), 0.0)
    store_taps(h3, 0, inside(hid, base3 - 3, c3, high3), c3)
    for r, n in chunks(10, 5):
        hid = jnp.maximum(conv(x2, r, n, c2, w[2], conv_bias[2:3]), 0.0)
        store_taps(h2, r, inside(hid, base2 - 3 + r, c2, high2), c2)
    path = conv(h3, 0, 6, c3, w[1], conv_bias[1:2]) + raw3[64:256]
    u = project(path.astype(BF), out_weight[0], out_bias[0:1])
    u = clamped(u[0:64], u[64:128], u[128:192], c3)
    for j in range(5):
        two = lift(table3[...], u[j * c3 : (j + 2) * c3])
        if j > 0:
            p2nd[2 * j - 1] = two[0:c2]
        if j < 4:
            p2nd[2 * j] = two[c2 : 2 * c2]

    raw2 = jnp.concatenate([m1[192:320], second[...], p1[64:192]], axis=0)
    for r, n in chunks(8, 4):
        lateral = conv(h2, r, n, c2, w[3], conv_bias[3:4])
        lateral = lateral + raw2[r * c2 : (r + n) * c2].astype(F32)
        joined = (lateral + p2nd[pl.ds(r, n)].reshape(n * c2, CH).astype(F32)).astype(BF)
        merged[pl.ds(r, n)] = joined.reshape(n, c2, CH)
        value = jnp.maximum(joined.astype(F32), 0.0)
        store_taps(x2, r, inside(value, base2 - 2 + r, c2, high2), c2)
    for r, n in chunks(6, 3):
        hid = jnp.maximum(conv(x2, r, n, c2, w[4], conv_bias[4:5]), 0.0)
        store_taps(h2, r, inside(hid, base2 - 1 + r, c2, high2), c2)
    refined = conv(h2, 0, 4, c2, w[5], conv_bias[5:6])
    refined = refined + merged[2:6].reshape(4 * c2, CH).astype(F32)
    kept[...] = project(refined.astype(BF), out_weight[1], out_bias[1:2])
    lower = first_half(1)
    start = [pl.multiple_of(jnp.where(lower == flag, 128, 0), 128) for flag in (True, False)]
    u_inner[...] = kept[pl.ds(start[0], 128)]
    u_outer[...] = kept[pl.ds(start[1], 128)]


def lateral_kernel(
    inner, outer, fine, w, conv_bias, h_mid, lat_top, lat_end, x_top, x_end, h_top, h_end,
):
    position = lax.axis_index("rows")
    ends = lax.axis_size("rows") - 1
    c1 = 128
    base, height = 8 * position, 8 * (ends + 1)
    mf, pf = sides(inner[...], outer[...], 1)
    raw_top = jnp.concatenate([mf, fine[0:256]], axis=0)
    raw_end = jnp.concatenate([fine[768:1024], pf], axis=0)
    h_top[5:7] = h_mid[0:2]
    h_end[0:2] = h_mid[4:6]
    for x, raw, first in ((x_top, raw_top, -5), (x_end, raw_end, 6)):
        for r, n in chunks(7, 4):
            value = jnp.maximum(raw[r * c1 : (r + n) * c1].astype(F32), 0.0)
            store_taps(x, r, inside(value, base + first + r, c1, height), c1)
    for x, h, first, at in ((x_top, h_top, -4, 0), (x_end, h_end, 7, 2)):
        hid = jnp.maximum(conv(x, 0, 5, c1, w[6], conv_bias[6:7]), 0.0)
        store_taps(h, at, inside(hid, base + first, c1, height), c1)
    for h, raw, skip, lateral in ((h_top, raw_top, 2, lat_top), (h_end, raw_end, 0, lat_end)):
        part = raw[skip * c1 : (skip + 5) * c1].astype(F32)
        lateral[...] = conv(h, 0, 5, c1, w[7], conv_bias[7:8]) + part


def fine_kernel(
    lat_top, lat_mid, lat_end, u_inner, u_outer, inner_u, outer_u, w, conv_bias, out_weight,
    out_bias, table2, table1, out, p1st, x1, hb, merged, u1, staged, sems,
):
    position = lax.axis_index("rows")
    ends = lax.axis_size("rows") - 1
    c2, c1 = 64, 128
    base, height = 8 * position, 8 * (ends + 1)
    mu, pu = sides(inner_u[...], outer_u[...], 1)
    above, below = sides(u_inner[...], u_outer[...], 1)
    u = clamped(mu, jnp.concatenate([above, below], axis=0), pu, c2)
    def merge(lateral, r, n, pairs):
        for j in pairs:
            two = lift(table2[...], u[j * c2 : (j + 2) * c2])
            p1st[2 * j : 2 * j + 2] = two.reshape(2, c1, CH)
        joined = (lateral[...] + p1st[pl.ds(r, n)].reshape(n * c1, CH).astype(F32)).astype(BF)
        merged[pl.ds(r, n)] = joined.reshape(n, c1, CH)
        value = jnp.maximum(joined.astype(F32), 0.0)
        store_taps(x1, r, inside(value, base - 3 + r, c1, height), c1)

    def hidden(r, n):
        hid = jnp.maximum(conv(x1, r, n, c1, w[8], conv_bias[8:9]), 0.0)
        store_taps(hb, r, inside(hid, base - 2 + r, c1, height), c1)

    merge(lat_top, 0, 5, range(0, 3))
    merge(lat_mid, 5, 4, range(3, 5))
    merge(lat_end, 9, 5, range(5, 7))
    hidden(0, 4)
    hidden(4, 4)
    hidden(8, 4)
    copies = []
    for r, n in chunks(10, 5):
        refined = conv(hb, r, n, c1, w[9], conv_bias[9:10])
        refined = refined + merged[pl.ds(r + 2, n)].reshape(n * c1, CH).astype(F32)
        u1[r * c1 : (r + n) * c1] = project(refined.astype(BF), out_weight[2], out_bias[2:3])
        edge, row, flag = (0, c1, 0) if r == 0 else (9 * c1, 8 * c1, ends)
        u1[edge : edge + c1] = jnp.where(
            position == flag, u1[row : row + c1], u1[edge : edge + c1]
        )
        for j in range(0, 4) if r == 0 else range(4, 9):
            first, count = max(2 * j - 1, 0), 2 if 0 < j < 8 else 1
            half = slice(2 * c1 if j == 0 else 0, 2 * c1 if j == 8 else 4 * c1)
            rows = lift(table1[half], u1[j * c1 : (j + 2) * c1])
            staged[pl.ds(first, count)] = rows.reshape(count, 2 * c1, CH)
            copies.append(
                pltpu.make_async_copy(
                    staged.at[pl.ds(first, count)], out.at[pl.ds(first, count)], sems.at[j]
                )
            )
            copies[-1].start()
    for copy in copies:
        copy.wait()


VM = pl.BlockSpec(memory_space=pltpu.VMEM)
ANY = pl.BlockSpec(memory_space=pltpu.HBM)


def call(kernel, in_vmem, in_hbm, outs, out_spec, scratch, sems, flops):
    return pl.pallas_call(
        kernel,
        out_shape=[jax.ShapeDtypeStruct(shape, kind) for shape, kind in outs],
        in_specs=[VM] * len(in_vmem) + [ANY] * len(in_hbm),
        out_specs=[out_spec] * len(outs),
        scratch_shapes=[pltpu.VMEM(shape, kind) for shape, kind in scratch]
        + [pltpu.SemaphoreType.DMA((sems,))] * (sems > 0),
        compiler_params=pltpu.CompilerParams(vmem_limit_bytes=VMEM_LIMIT),
        cost_estimate=pl.CostEstimate(flops=flops, bytes_accessed=1_000_000, transcendentals=0),
    )(*in_vmem, *(pltpu.with_memory_space_constraint(x, pltpu.HBM) for x in in_hbm))


def local(feat_fine, feat_second, feat_third, conv_weight, conv_bias, out_weight, out_bias):
    devices = lax.axis_size("rows")

    def exchange(value_in, value_out, hop):
        values = (value_in, value_out)
        pairs = pair_up(hop, devices, lax.axis_size("img"))
        return [lax.ppermute(v, ("img", "rows"), p) for v, p in zip(values, pairs)]

    third = feat_third.reshape(64, CH)
    second = feat_second.reshape(256, CH)
    fine = feat_fine.reshape(1024, CH)
    weight = conv_weight.reshape(10, TAPS, CH)
    pack, fine_in, fine_out = call(
        pack_kernel,
        (),
        (third, second, fine),
        [((320, CH), BF), ((640, CH), BF), ((640, CH), BF)],
        VM,
        [],
        4,
        PACK_COST,
    )
    near = exchange(pack, pack, 1)
    far = exchange(third, third, 2)
    h_mid, lat_mid = call(
        middle_kernel,
        (fine, weight, conv_bias),
        (),
        [((6, 128, 3 * CH), BF), ((512, CH), F32)],
        VM,
        [((8, 128, 3 * CH), BF)],
        0,
        FETCH_COST,
    )
    halo = exchange(fine_in, fine_out, 1)
    u2 = call(
        coarse_kernel,
        (*near, *far, second, third, weight, conv_bias, out_weight, out_bias, pair_table(32)),
        (),
        [((128, CH), BF)] * 2,
        VM,
        [
            ((10, 32, 3 * CH), BF),
            ((8, 32, 3 * CH), BF),
            ((12, 64, 3 * CH), BF),
            ((10, 64, 3 * CH), BF),
            ((8, 64, CH), BF),
            ((8, 64, CH), BF),
            ((256, CH), BF),
        ],
        0,
        4_000_000_000,
    )
    got = exchange(*u2, 1)
    lat_top, lat_end = call(
        lateral_kernel,
        (*halo, fine, weight, conv_bias, h_mid),
        (),
        [((640, CH), F32)] * 2,
        VM,
        [((7, 128, 3 * CH), BF)] * 4,
        0,
        4_000_000_000,
    )
    (out,) = call(
        fine_kernel,
        (
            lat_top, lat_mid, lat_end, *u2, *got, weight, conv_bias, out_weight, out_bias,
            pair_table(64), pair_table(128),
        ),
        (),
        [((16, 256, CH), BF)],
        ANY,
        [
            ((14, 128, CH), BF),
            ((14, 128, 3 * CH), BF),
            ((12, 128, 3 * CH), BF),
            ((14, 128, CH), BF),
            ((1280, CH), BF),
            ((16, 256, CH), BF),
        ],
        9,
        4_000_000_000,
    )
    return out


def solution(mesh):
    rows = P(("img", "rows"), None, None)
    return jax.shard_map(
        local,
        mesh=mesh,
        in_specs=(rows, rows, rows, P(), P(), P(), P()),
        out_specs=rows,
        check_vma=False,
    )
```

```python
import functools

import jax
import jax.numpy as jnp
import numpy as np
from jax import lax
from jax.experimental import pallas as pl
from jax.experimental.pallas import tpu as pltpu
from jax.sharding import PartitionSpec as P

CH = 256
TAPS = 9 * CH
BF = jnp.bfloat16
F32 = jnp.float32
FETCH_COST = 20_000_000_000
PACK_COST = 20_000_000_000
VMEM_LIMIT = 20 * 1024 * 1024


def pair_table(columns):
    cols = np.zeros((2 * columns, columns), np.float32)
    for m in range(columns):
        cols[2 * m, max(m - 1, 0)] += 0.25
        cols[2 * m, m] += 0.75
        cols[2 * m + 1, m] += 0.75
        cols[2 * m + 1, min(m + 1, columns - 1)] += 0.25
    table = np.block([[0.75 * cols, 0.25 * cols], [0.25 * cols, 0.75 * cols]])
    return jnp.asarray(table, BF)


def store_taps(dst, row, value, columns):
    cells = value.shape[0]
    rows = cells // columns
    column = lax.broadcasted_iota(jnp.int32, (cells, 1), 0) % columns
    left = jnp.where(column == 0, 0.0, pltpu.roll(value, 1, 0))
    right = jnp.where(column == columns - 1, 0.0, pltpu.roll(value, cells - 1, 0))
    for part, piece in enumerate((left, value, right)):
        dst[pl.ds(row, rows), :, part * CH : (part + 1) * CH] = piece.astype(BF).reshape(
            rows, columns, CH
        )


def conv(src, row, rows, columns, weight, bias):
    lhs = jnp.concatenate(
        [src[pl.ds(row + a, rows)].reshape(rows * columns, 3 * CH) for a in range(3)], axis=1
    )
    return jnp.dot(lhs, weight, preferred_element_type=F32) + bias


def inside(value, first, columns, height):
    cells = value.shape[0]
    row = first + lax.broadcasted_iota(jnp.int32, (cells, 1), 0) // columns
    return jnp.where((row >= 0) & (row < height), value, 0.0)


def chunks(rows, step):
    return [(r, min(step, rows - r)) for r in range(0, rows, step)]


def project(cells, weight, bias):
    return (jnp.dot(cells, weight, preferred_element_type=F32) + bias).astype(BF)


def lift(table, cells):
    return jnp.dot(table, cells, preferred_element_type=F32).astype(BF)


def load(sems, *pairs):
    copies = [pltpu.make_async_copy(src, dst, sems.at[k]) for k, (src, dst) in enumerate(pairs)]
    for copy in copies:
        copy.start()
    return copies


def pair_up(hop, devices, parts):
    inner = [i ^ hop for i in range(devices)]
    outer = [((i - hop) ^ hop) + hop for i in range(devices)]
    return [
        [
            (p * devices + i, p * devices + j if 0 <= j < devices else (p ^ 1) * devices + i)
            for p in range(parts)
            for i, j in enumerate(ends)
        ]
        for ends in (inner, outer)
    ]


def first_half(hop):
    return (lax.axis_index("rows") // hop) % 2 == 0


def sides(inner, outer, hop):
    lower = first_half(hop)
    return jnp.where(lower, outer, inner), jnp.where(lower, inner, outer)


def edge_rows(fine, flag):
    start = jnp.where(first_half(1) == flag, 384, 0)
    return fine.at[pl.ds(pl.multiple_of(start, 128), 640)]


def pack_kernel(third, second, fine, pack, inner, outer, far, sems):
    copies = load(
        sems,
        (edge_rows(fine, True), inner),
        (edge_rows(fine, False), outer),
        (second, pack.at[pl.ds(64, 256)]),
        (third, pack.at[pl.ds(0, 64)]),
        (third, far),
    )
    for copy in copies:
        copy.wait()


def middle_kernel(fine, w, conv_bias, h_mid, lat_mid, x1):
    c1 = 128
    for r in (0, 4):
        store_taps(x1, r, jnp.maximum(fine[r * c1 : (r + 4) * c1].astype(F32), 0.0), c1)
    for r, n in chunks(6, 3):
        hid = jnp.maximum(conv(x1, r, n, c1, w[6], conv_bias[6:7]), 0.0)
        store_taps(h_mid, r, hid, c1)
    lat_mid[...] = conv(h_mid, 0, 4, c1, w[7], conv_bias[7:8]) + fine[2 * c1 : 6 * c1].astype(F32)


def clamped(above, own, below, columns):
    position = lax.axis_index("rows")
    ends = lax.axis_size("rows") - 1
    last = above.shape[0] - columns
    above_row = jnp.where(position == 0, own[0:columns], above[last:])
    below_row = jnp.where(position == ends, own[own.shape[0] - columns :], below[0:columns])
    return jnp.concatenate([above[0:last], above_row, own, below_row, below[columns:]], axis=0)


def coarse_kernel(
    inner2, outer2, inner1, outer1, second, third, w, conv_bias, out_weight, out_bias, table3,
    u_inner, u_outer, x3, h3, x2, h2, p2nd, merged, kept,
):
    position = lax.axis_index("rows")
    ends = lax.axis_size("rows") - 1
    c3, c2 = 32, 64
    base3, base2 = 2 * position, 4 * position
    high3, high2 = 2 * (ends + 1), 4 * (ends + 1)
    m1, p1 = sides(inner1[...], outer1[...], 1)
    m2, p2 = sides(inner2[...], outer2[...], 2)

    raw3 = jnp.concatenate([m2, m1[0:64], third[...], p1[0:64], p2], axis=0).astype(F32)
    store_taps(x3, 0, inside(jnp.maximum(raw3, 0.0), base3 - 4, c3, high3), c3)
    for row, part in ((0, m1[64:320]), (4, second[...]), (8, p1[64:320])):
        value = jnp.maximum(part.astype(F32), 0.0)
        store_taps(x2, row, inside(value, base2 + row - 4, c2, high2), c2)

    hid = jnp.maximum(conv(x3, 0, 8, c3, w[0], conv_bias[0:1]), 0.0)
    store_taps(h3, 0, inside(hid, base3 - 3, c3, high3), c3)
    for r, n in chunks(10, 5):
        hid = jnp.maximum(conv(x2, r, n, c2, w[2], conv_bias[2:3]), 0.0)
        store_taps(h2, r, inside(hid, base2 - 3 + r, c2, high2), c2)
    path = conv(h3, 0, 6, c3, w[1], conv_bias[1:2]) + raw3[64:256]
    u = project(path.astype(BF), out_weight[0], out_bias[0:1])
    u = clamped(u[0:64], u[64:128], u[128:192], c3)
    for j in range(5):
        two = lift(table3[...], u[j * c3 : (j + 2) * c3])
        if j > 0:
            p2nd[2 * j - 1] = two[0:c2]
        if j < 4:
            p2nd[2 * j] = two[c2 : 2 * c2]

    raw2 = jnp.concatenate([m1[192:320], second[...], p1[64:192]], axis=0)
    for r, n in chunks(8, 4):
        lateral = conv(h2, r, n, c2, w[3], conv_bias[3:4])
        lateral = lateral + raw2[r * c2 : (r + n) * c2].astype(F32)
        joined = (lateral + p2nd[pl.ds(r, n)].reshape(n * c2, CH).astype(F32)).astype(BF)
        merged[pl.ds(r, n)] = joined.reshape(n, c2, CH)
        value = jnp.maximum(joined.astype(F32), 0.0)
        store_taps(x2, r, inside(value, base2 - 2 + r, c2, high2), c2)
    for r, n in chunks(6, 3):
        hid = jnp.maximum(conv(x2, r, n, c2, w[4], conv_bias[4:5]), 0.0)
        store_taps(h2, r, inside(hid, base2 - 1 + r, c2, high2), c2)
    refined = conv(h2, 0, 4, c2, w[5], conv_bias[5:6])
    refined = refined + merged[2:6].reshape(4 * c2, CH).astype(F32)
    kept[...] = project(refined.astype(BF), out_weight[1], out_bias[1:2])
    lower = first_half(1)
    start = [pl.multiple_of(jnp.where(lower == flag, 128, 0), 128) for flag in (True, False)]
    u_inner[...] = kept[pl.ds(start[0], 128)]
    u_outer[...] = kept[pl.ds(start[1], 128)]


def lateral_kernel(
    inner, outer, fine, w, conv_bias, h_mid, lat_top, lat_end, x_top, x_end, h_top, h_end,
):
    position = lax.axis_index("rows")
    ends = lax.axis_size("rows") - 1
    c1 = 128
    base, height = 8 * position, 8 * (ends + 1)
    mf, pf = sides(inner[...], outer[...], 1)
    raw_top = jnp.concatenate([mf, fine[0:256]], axis=0)
    raw_end = jnp.concatenate([fine[768:1024], pf], axis=0)
    h_top[5:7] = h_mid[0:2]
    h_end[0:2] = h_mid[4:6]
    for x, raw, first in ((x_top, raw_top, -5), (x_end, raw_end, 6)):
        for r, n in chunks(7, 4):
            value = jnp.maximum(raw[r * c1 : (r + n) * c1].astype(F32), 0.0)
            store_taps(x, r, inside(value, base + first + r, c1, height), c1)
    for x, h, first, at in ((x_top, h_top, -4, 0), (x_end, h_end, 7, 2)):
        hid = jnp.maximum(conv(x, 0, 5, c1, w[6], conv_bias[6:7]), 0.0)
        store_taps(h, at, inside(hid, base + first, c1, height), c1)
    for h, raw, skip, lateral in ((h_top, raw_top, 2, lat_top), (h_end, raw_end, 0, lat_end)):
        part = raw[skip * c1 : (skip + 5) * c1].astype(F32)
        lateral[...] = conv(h, 0, 5, c1, w[7], conv_bias[7:8]) + part


def fine_kernel(
    lat_top, lat_mid, lat_end, u_inner, u_outer, inner_u, outer_u, w, conv_bias, out_weight,
    out_bias, table2, table1, out, p1st, x1, hb, merged, u1, staged, sems,
):
    position = lax.axis_index("rows")
    ends = lax.axis_size("rows") - 1
    c2, c1 = 64, 128
    base, height = 8 * position, 8 * (ends + 1)
    mu, pu = sides(inner_u[...], outer_u[...], 1)
    above, below = sides(u_inner[...], u_outer[...], 1)
    u = clamped(mu, jnp.concatenate([above, below], axis=0), pu, c2)
    def merge(lateral, r, n, pairs):
        for j in pairs:
            two = lift(table2[...], u[j * c2 : (j + 2) * c2])
            p1st[2 * j : 2 * j + 2] = two.reshape(2, c1, CH)
        joined = (lateral[...] + p1st[pl.ds(r, n)].reshape(n * c1, CH).astype(F32)).astype(BF)
        merged[pl.ds(r, n)] = joined.reshape(n, c1, CH)
        value = jnp.maximum(joined.astype(F32), 0.0)
        store_taps(x1, r, inside(value, base - 3 + r, c1, height), c1)

    def hidden(r, n):
        hid = jnp.maximum(conv(x1, r, n, c1, w[8], conv_bias[8:9]), 0.0)
        store_taps(hb, r, inside(hid, base - 2 + r, c1, height), c1)

    merge(lat_top, 0, 5, range(0, 3))
    merge(lat_mid, 5, 4, range(3, 5))
    merge(lat_end, 9, 5, range(5, 7))
    hidden(0, 4)
    hidden(4, 4)
    hidden(8, 4)
    copies = []
    for r, n in chunks(10, 5):
        refined = conv(hb, r, n, c1, w[9], conv_bias[9:10])
        refined = refined + merged[pl.ds(r + 2, n)].reshape(n * c1, CH).astype(F32)
        u1[r * c1 : (r + n) * c1] = project(refined.astype(BF), out_weight[2], out_bias[2:3])
        edge, row, flag = (0, c1, 0) if r == 0 else (9 * c1, 8 * c1, ends)
        u1[edge : edge + c1] = jnp.where(
            position == flag, u1[row : row + c1], u1[edge : edge + c1]
        )
        for j in range(0, 4) if r == 0 else range(4, 9):
            first, count = max(2 * j - 1, 0), 2 if 0 < j < 8 else 1
            half = slice(2 * c1 if j == 0 else 0, 2 * c1 if j == 8 else 4 * c1)
            rows = lift(table1[half], u1[j * c1 : (j + 2) * c1])
            staged[pl.ds(first, count)] = rows.reshape(count, 2 * c1, CH)
            copies.append(
                pltpu.make_async_copy(
                    staged.at[pl.ds(first, count)], out.at[pl.ds(first, count)], sems.at[j]
                )
            )
            copies[-1].start()
    for copy in copies:
        copy.wait()


VM = pl.BlockSpec(memory_space=pltpu.VMEM)
ANY = pl.BlockSpec(memory_space=pltpu.HBM)


def call(kernel, in_vmem, in_hbm, outs, out_spec, scratch, sems, flops):
    return pl.pallas_call(
        kernel,
        out_shape=[jax.ShapeDtypeStruct(shape, kind) for shape, kind in outs],
        in_specs=[VM] * len(in_vmem) + [ANY] * len(in_hbm),
        out_specs=[out_spec] * len(outs),
        scratch_shapes=[pltpu.VMEM(shape, kind) for shape, kind in scratch]
        + [pltpu.SemaphoreType.DMA((sems,))] * (sems > 0),
        compiler_params=pltpu.CompilerParams(vmem_limit_bytes=VMEM_LIMIT),
        cost_estimate=pl.CostEstimate(flops=flops, bytes_accessed=1_000_000, transcendentals=0),
    )(*in_vmem, *(pltpu.with_memory_space_constraint(x, pltpu.HBM) for x in in_hbm))


def local(feat_fine, feat_second, feat_third, conv_weight, conv_bias, out_weight, out_bias):
    devices = lax.axis_size("rows")

    def exchange(value_in, value_out, hop):
        values = (value_in, value_out)
        pairs = pair_up(hop, devices, lax.axis_size("img"))
        return [lax.ppermute(v, ("img", "rows"), p) for v, p in zip(values, pairs)]

    third = feat_third.reshape(64, CH)
    second = feat_second.reshape(256, CH)
    fine = feat_fine.reshape(1024, CH)
    weight = conv_weight.reshape(10, TAPS, CH)
    pack, fine_in, fine_out, third_out = call(
        pack_kernel,
        (),
        (third, second, fine),
        [((320, CH), BF), ((640, CH), BF), ((640, CH), BF), ((64, CH), BF)],
        VM,
        [],
        5,
        PACK_COST,
    )
    far = exchange(third_out, third_out, 2)
    near = exchange(pack, pack, 1)
    h_mid, lat_mid = call(
        middle_kernel,
        (fine, weight, conv_bias),
        (),
        [((6, 128, 3 * CH), BF), ((512, CH), F32)],
        VM,
        [((8, 128, 3 * CH), BF)],
        0,
        FETCH_COST,
    )
    halo = exchange(fine_in, fine_out, 1)
    u2 = call(
        coarse_kernel,
        (*far, *near, second, third, weight, conv_bias, out_weight, out_bias, pair_table(32)),
        (),
        [((128, CH), BF)] * 2,
        VM,
        [
            ((10, 32, 3 * CH), BF),
            ((8, 32, 3 * CH), BF),
            ((12, 64, 3 * CH), BF),
            ((10, 64, 3 * CH), BF),
            ((8, 64, CH), BF),
            ((8, 64, CH), BF),
            ((256, CH), BF),
        ],
        0,
        4_000_000_000,
    )
    got = exchange(*u2, 1)
    lat_top, lat_end = call(
        lateral_kernel,
        (*halo, fine, weight, conv_bias, h_mid),
        (),
        [((640, CH), F32)] * 2,
        VM,
        [((7, 128, 3 * CH), BF)] * 4,
        0,
        4_000_000_000,
    )
    (out,) = call(
        fine_kernel,
        (
            lat_top, lat_mid, lat_end, *u2, *got, weight, conv_bias, out_weight, out_bias,
            pair_table(64), pair_table(128),
        ),
        (),
        [((16, 256, CH), BF)],
        ANY,
        [
            ((14, 128, CH), BF),
            ((14, 128, 3 * CH), BF),
            ((12, 128, 3 * CH), BF),
            ((14, 128, CH), BF),
            ((1280, CH), BF),
            ((16, 256, CH), BF),
        ],
        9,
        4_000_000_000,
    )
    return out


def solution(mesh):
    rows = P(("img", "rows"), None, None)
    return jax.shard_map(
        local,
        mesh=mesh,
        in_specs=(rows, rows, rows, P(), P(), P(), P()),
        out_specs=rows,
        check_vma=False,
    )
```

```python
import functools

import jax
import jax.numpy as jnp
import numpy as np
from jax import lax
from jax.experimental import pallas as pl
from jax.experimental.pallas import tpu as pltpu
from jax.sharding import PartitionSpec as P

CH = 256
TAPS = 9 * CH
BF = jnp.bfloat16
F32 = jnp.float32
FETCH_COST = 20_000_000_000
PACK_COST = 20_000_000_000
VMEM_LIMIT = 20 * 1024 * 1024


def pair_table(columns):
    cols = np.zeros((2 * columns, columns), np.float32)
    for m in range(columns):
        cols[2 * m, max(m - 1, 0)] += 0.25
        cols[2 * m, m] += 0.75
        cols[2 * m + 1, m] += 0.75
        cols[2 * m + 1, min(m + 1, columns - 1)] += 0.25
    table = np.block([[0.75 * cols, 0.25 * cols], [0.25 * cols, 0.75 * cols]])
    return jnp.asarray(table, BF)


def store_taps(dst, row, value, columns):
    cells = value.shape[0]
    rows = cells // columns
    column = lax.broadcasted_iota(jnp.int32, (cells, 1), 0) % columns
    left = jnp.where(column == 0, 0.0, pltpu.roll(value, 1, 0))
    right = jnp.where(column == columns - 1, 0.0, pltpu.roll(value, cells - 1, 0))
    for part, piece in enumerate((left, value, right)):
        dst[pl.ds(row, rows), :, part * CH : (part + 1) * CH] = piece.astype(BF).reshape(
            rows, columns, CH
        )


def conv(src, row, rows, columns, weight, bias):
    lhs = jnp.concatenate(
        [src[pl.ds(row + a, rows)].reshape(rows * columns, 3 * CH) for a in range(3)], axis=1
    )
    return jnp.dot(lhs, weight, preferred_element_type=F32) + bias


def inside(value, first, columns, height):
    cells = value.shape[0]
    row = first + lax.broadcasted_iota(jnp.int32, (cells, 1), 0) // columns
    return jnp.where((row >= 0) & (row < height), value, 0.0)


def chunks(rows, step):
    return [(r, min(step, rows - r)) for r in range(0, rows, step)]


def project(cells, weight, bias):
    return (jnp.dot(cells, weight, preferred_element_type=F32) + bias).astype(BF)


def lift(table, cells):
    return jnp.dot(table, cells, preferred_element_type=F32).astype(BF)


def load(sems, *pairs):
    copies = [pltpu.make_async_copy(src, dst, sems.at[k]) for k, (src, dst) in enumerate(pairs)]
    for copy in copies:
        copy.start()
    return copies


def pair_up(hop, devices, parts):
    inner = [i ^ hop for i in range(devices)]
    outer = [((i - hop) ^ hop) + hop for i in range(devices)]
    return [
        [
            (p * devices + i, p * devices + j if 0 <= j < devices else (p ^ 1) * devices + i)
            for p in range(parts)
            for i, j in enumerate(ends)
        ]
        for ends in (inner, outer)
    ]


def first_half(hop):
    return (lax.axis_index("rows") // hop) % 2 == 0


def sides(inner, outer, hop):
    lower = first_half(hop)
    return jnp.where(lower, outer, inner), jnp.where(lower, inner, outer)


def edge_rows(fine, flag):
    start = jnp.where(first_half(1) == flag, 384, 0)
    return fine.at[pl.ds(pl.multiple_of(start, 128), 640)]


def pack_kernel(third, second, fine, pack, inner, outer, far, sems):
    copies = load(
        sems,
        (edge_rows(fine, True), inner),
        (edge_rows(fine, False), outer),
        (second, pack.at[pl.ds(64, 256)]),
        (third, pack.at[pl.ds(0, 64)]),
        (third, far),
    )
    for copy in copies:
        copy.wait()


def middle_kernel(fine, w, conv_bias, h_mid, lat_mid, x1):
    c1 = 128
    for r in (0, 4):
        store_taps(x1, r, jnp.maximum(fine[r * c1 : (r + 4) * c1].astype(F32), 0.0), c1)
    for r, n in chunks(6, 3):
        hid = jnp.maximum(conv(x1, r, n, c1, w[6], conv_bias[6:7]), 0.0)
        store_taps(h_mid, r, hid, c1)
    lat_mid[...] = conv(h_mid, 0, 4, c1, w[7], conv_bias[7:8]) + fine[2 * c1 : 6 * c1].astype(F32)


def clamped(above, own, below, columns):
    position = lax.axis_index("rows")
    ends = lax.axis_size("rows") - 1
    last = above.shape[0] - columns
    above_row = jnp.where(position == 0, own[0:columns], above[last:])
    below_row = jnp.where(position == ends, own[own.shape[0] - columns :], below[0:columns])
    return jnp.concatenate([above[0:last], above_row, own, below_row, below[columns:]], axis=0)


def coarse_kernel(
    inner2, outer2, inner1, outer1, second, third, w, conv_bias, out_weight, out_bias, table3,
    u_inner, u_outer, x3, h3, x2, h2, p2nd, merged, kept,
):
    position = lax.axis_index("rows")
    ends = lax.axis_size("rows") - 1
    c3, c2 = 32, 64
    base3, base2 = 2 * position, 4 * position
    high3, high2 = 2 * (ends + 1), 4 * (ends + 1)
    m1, p1 = sides(inner1[...], outer1[...], 1)
    m2, p2 = sides(inner2[...], outer2[...], 2)

    raw3 = jnp.concatenate([m2, m1[0:64], third[...], p1[0:64], p2], axis=0).astype(F32)
    store_taps(x3, 0, inside(jnp.maximum(raw3, 0.0), base3 - 4, c3, high3), c3)
    for row, part in ((0, m1[64:320]), (4, second[...]), (8, p1[64:320])):
        value = jnp.maximum(part.astype(F32), 0.0)
        store_taps(x2, row, inside(value, base2 + row - 4, c2, high2), c2)

    hid = jnp.maximum(conv(x3, 0, 8, c3, w[0], conv_bias[0:1]), 0.0)
    store_taps(h3, 0, inside(hid, base3 - 3, c3, high3), c3)
    for r, n in chunks(10, 5):
        hid = jnp.maximum(conv(x2, r, n, c2, w[2], conv_bias[2:3]), 0.0)
        store_taps(h2, r, inside(hid, base2 - 3 + r, c2, high2), c2)
    path = conv(h3, 0, 6, c3, w[1], conv_bias[1:2]) + raw3[64:256]
    u = project(path.astype(BF), out_weight[0], out_bias[0:1])
    u = clamped(u[0:64], u[64:128], u[128:192], c3)
    for j in range(5):
        two = lift(table3[...], u[j * c3 : (j + 2) * c3])
        if j > 0:
            p2nd[2 * j - 1] = two[0:c2]
        if j < 4:
            p2nd[2 * j] = two[c2 : 2 * c2]

    raw2 = jnp.concatenate([m1[192:320], second[...], p1[64:192]], axis=0)
    for r, n in chunks(8, 2):
        lateral = conv(h2, r, n, c2, w[3], conv_bias[3:4])
        lateral = lateral + raw2[r * c2 : (r + n) * c2].astype(F32)
        joined = (lateral + p2nd[pl.ds(r, n)].reshape(n * c2, CH).astype(F32)).astype(BF)
        merged[pl.ds(r, n)] = joined.reshape(n, c2, CH)
        value = jnp.maximum(joined.astype(F32), 0.0)
        store_taps(x2, r, inside(value, base2 - 2 + r, c2, high2), c2)
    for r, n in chunks(6, 2):
        hid = jnp.maximum(conv(x2, r, n, c2, w[4], conv_bias[4:5]), 0.0)
        store_taps(h2, r, inside(hid, base2 - 1 + r, c2, high2), c2)
    for r, n in chunks(4, 2):
        refined = conv(h2, r, n, c2, w[5], conv_bias[5:6])
        refined = refined + merged[r + 2 : r + 2 + n].reshape(n * c2, CH).astype(F32)
        kept[r * c2 : (r + n) * c2] = project(
            refined.astype(BF), out_weight[1], out_bias[1:2]
        )
    lower = first_half(1)
    start = [pl.multiple_of(jnp.where(lower == flag, 128, 0), 128) for flag in (True, False)]
    u_inner[...] = kept[pl.ds(start[0], 128)]
    u_outer[...] = kept[pl.ds(start[1], 128)]


def lateral_kernel(
    inner, outer, fine, w, conv_bias, h_mid, lat_top, lat_end, x_top, x_end, h_top, h_end,
):
    position = lax.axis_index("rows")
    ends = lax.axis_size("rows") - 1
    c1 = 128
    base, height = 8 * position, 8 * (ends + 1)
    mf, pf = sides(inner[...], outer[...], 1)
    raw_top = jnp.concatenate([mf, fine[0:256]], axis=0)
    raw_end = jnp.concatenate([fine[768:1024], pf], axis=0)
    h_top[5:7] = h_mid[0:2]
    h_end[0:2] = h_mid[4:6]
    for x, raw, first in ((x_top, raw_top, -5), (x_end, raw_end, 6)):
        for r, n in chunks(7, 4):
            value = jnp.maximum(raw[r * c1 : (r + n) * c1].astype(F32), 0.0)
            store_taps(x, r, inside(value, base + first + r, c1, height), c1)
    for x, h, first, at in ((x_top, h_top, -4, 0), (x_end, h_end, 7, 2)):
        for r, n in chunks(5, 3):
            hid = jnp.maximum(conv(x, r, n, c1, w[6], conv_bias[6:7]), 0.0)
            store_taps(h, at + r, inside(hid, base + first + r, c1, height), c1)
    for h, raw, skip, lateral in ((h_top, raw_top, 2, lat_top), (h_end, raw_end, 0, lat_end)):
        part = raw[skip * c1 : (skip + 5) * c1].astype(F32)
        lateral[...] = conv(h, 0, 5, c1, w[7], conv_bias[7:8]) + part


def fine_kernel(
    lat_top, lat_mid, lat_end, u_inner, u_outer, inner_u, outer_u, w, conv_bias, out_weight,
    out_bias, table2, table1, out, p1st, x1, hb, merged, u1, staged, sems,
):
    position = lax.axis_index("rows")
    ends = lax.axis_size("rows") - 1
    c2, c1 = 64, 128
    base, height = 8 * position, 8 * (ends + 1)
    mu, pu = sides(inner_u[...], outer_u[...], 1)
    above, below = sides(u_inner[...], u_outer[...], 1)
    u = clamped(mu, jnp.concatenate([above, below], axis=0), pu, c2)
    def merge(lateral, r, n, pairs):
        for j in pairs:
            two = lift(table2[...], u[j * c2 : (j + 2) * c2])
            p1st[2 * j : 2 * j + 2] = two.reshape(2, c1, CH)
        joined = (lateral[...] + p1st[pl.ds(r, n)].reshape(n * c1, CH).astype(F32)).astype(BF)
        merged[pl.ds(r, n)] = joined.reshape(n, c1, CH)
        value = jnp.maximum(joined.astype(F32), 0.0)
        store_taps(x1, r, inside(value, base - 3 + r, c1, height), c1)

    def hidden(r, n):
        hid = jnp.maximum(conv(x1, r, n, c1, w[8], conv_bias[8:9]), 0.0)
        store_taps(hb, r, inside(hid, base - 2 + r, c1, height), c1)

    merge(lat_top, 0, 5, range(0, 3))
    merge(lat_mid, 5, 4, range(3, 5))
    merge(lat_end, 9, 5, range(5, 7))
    hidden(0, 4)
    hidden(4, 4)
    hidden(8, 4)
    copies = []
    for r, n in chunks(10, 5):
        refined = conv(hb, r, n, c1, w[9], conv_bias[9:10])
        refined = refined + merged[pl.ds(r + 2, n)].reshape(n * c1, CH).astype(F32)
        u1[r * c1 : (r + n) * c1] = project(refined.astype(BF), out_weight[2], out_bias[2:3])
        edge, row, flag = (0, c1, 0) if r == 0 else (9 * c1, 8 * c1, ends)
        u1[edge : edge + c1] = jnp.where(
            position == flag, u1[row : row + c1], u1[edge : edge + c1]
        )
        for j in range(0, 4) if r == 0 else range(4, 9):
            first, count = max(2 * j - 1, 0), 2 if 0 < j < 8 else 1
            half = slice(2 * c1 if j == 0 else 0, 2 * c1 if j == 8 else 4 * c1)
            rows = lift(table1[half], u1[j * c1 : (j + 2) * c1])
            staged[pl.ds(first, count)] = rows.reshape(count, 2 * c1, CH)
            copies.append(
                pltpu.make_async_copy(
                    staged.at[pl.ds(first, count)], out.at[pl.ds(first, count)], sems.at[j]
                )
            )
            copies[-1].start()
    for copy in copies:
        copy.wait()


VM = pl.BlockSpec(memory_space=pltpu.VMEM)
ANY = pl.BlockSpec(memory_space=pltpu.HBM)


def call(kernel, in_vmem, in_hbm, outs, out_spec, scratch, sems, flops):
    return pl.pallas_call(
        kernel,
        out_shape=[jax.ShapeDtypeStruct(shape, kind) for shape, kind in outs],
        in_specs=[VM] * len(in_vmem) + [ANY] * len(in_hbm),
        out_specs=[out_spec] * len(outs),
        scratch_shapes=[pltpu.VMEM(shape, kind) for shape, kind in scratch]
        + [pltpu.SemaphoreType.DMA((sems,))] * (sems > 0),
        compiler_params=pltpu.CompilerParams(vmem_limit_bytes=VMEM_LIMIT),
        cost_estimate=pl.CostEstimate(flops=flops, bytes_accessed=1_000_000, transcendentals=0),
    )(*in_vmem, *(pltpu.with_memory_space_constraint(x, pltpu.HBM) for x in in_hbm))


def local(feat_fine, feat_second, feat_third, conv_weight, conv_bias, out_weight, out_bias):
    devices = lax.axis_size("rows")

    def exchange(value_in, value_out, hop):
        values = (value_in, value_out)
        pairs = pair_up(hop, devices, lax.axis_size("img"))
        return [lax.ppermute(v, ("img", "rows"), p) for v, p in zip(values, pairs)]

    third = feat_third.reshape(64, CH)
    second = feat_second.reshape(256, CH)
    fine = feat_fine.reshape(1024, CH)
    weight = conv_weight.reshape(10, TAPS, CH)
    pack, fine_in, fine_out, third_out = call(
        pack_kernel,
        (),
        (third, second, fine),
        [((320, CH), BF), ((640, CH), BF), ((640, CH), BF), ((64, CH), BF)],
        VM,
        [],
        5,
        PACK_COST,
    )
    far = exchange(third_out, third_out, 2)
    near = exchange(pack, pack, 1)
    h_mid, lat_mid = call(
        middle_kernel,
        (fine, weight, conv_bias),
        (),
        [((6, 128, 3 * CH), BF), ((512, CH), F32)],
        VM,
        [((8, 128, 3 * CH), BF)],
        0,
        FETCH_COST,
    )
    halo = exchange(fine_in, fine_out, 1)
    u2 = call(
        coarse_kernel,
        (*far, *near, second, third, weight, conv_bias, out_weight, out_bias, pair_table(32)),
        (),
        [((128, CH), BF)] * 2,
        VM,
        [
            ((10, 32, 3 * CH), BF),
            ((8, 32, 3 * CH), BF),
            ((12, 64, 3 * CH), BF),
            ((10, 64, 3 * CH), BF),
            ((8, 64, CH), BF),
            ((8, 64, CH), BF),
            ((256, CH), BF),
        ],
        0,
        4_000_000_000,
    )
    got = exchange(*u2, 1)
    lat_top, lat_end = call(
        lateral_kernel,
        (*halo, fine, weight, conv_bias, h_mid),
        (),
        [((640, CH), F32)] * 2,
        VM,
        [((7, 128, 3 * CH), BF)] * 4,
        0,
        4_000_000_000,
    )
    (out,) = call(
        fine_kernel,
        (
            lat_top, lat_mid, lat_end, *u2, *got, weight, conv_bias, out_weight, out_bias,
            pair_table(64), pair_table(128),
        ),
        (),
        [((16, 256, CH), BF)],
        ANY,
        [
            ((14, 128, CH), BF),
            ((14, 128, 3 * CH), BF),
            ((12, 128, 3 * CH), BF),
            ((14, 128, CH), BF),
            ((1280, CH), BF),
            ((16, 256, CH), BF),
        ],
        9,
        4_000_000_000,
    )
    return out


def solution(mesh):
    rows = P(("img", "rows"), None, None)
    return jax.shard_map(
        local,
        mesh=mesh,
        in_specs=(rows, rows, rows, P(), P(), P(), P()),
        out_specs=rows,
        check_vma=False,
    )
```

```python
import functools

import jax
import jax.numpy as jnp
import numpy as np
from jax import lax
from jax.experimental import pallas as pl
from jax.experimental.pallas import tpu as pltpu
from jax.sharding import PartitionSpec as P

CH = 256
TAPS = 9 * CH
BF = jnp.bfloat16
F32 = jnp.float32
FETCH_COST = 20_000_000_000
PACK_COST = 20_000_000_000
VMEM_LIMIT = 20 * 1024 * 1024


def pair_table(columns):
    cols = np.zeros((2 * columns, columns), np.float32)
    for m in range(columns):
        cols[2 * m, max(m - 1, 0)] += 0.25
        cols[2 * m, m] += 0.75
        cols[2 * m + 1, m] += 0.75
        cols[2 * m + 1, min(m + 1, columns - 1)] += 0.25
    table = np.block([[0.75 * cols, 0.25 * cols], [0.25 * cols, 0.75 * cols]])
    return jnp.asarray(table, BF)


def store_taps(dst, row, value, columns):
    cells = value.shape[0]
    rows = cells // columns
    column = lax.broadcasted_iota(jnp.int32, (cells, 1), 0) % columns
    left = jnp.where(column == 0, 0.0, pltpu.roll(value, 1, 0))
    right = jnp.where(column == columns - 1, 0.0, pltpu.roll(value, cells - 1, 0))
    for part, piece in enumerate((left, value, right)):
        dst[pl.ds(row, rows), :, part * CH : (part + 1) * CH] = piece.astype(BF).reshape(
            rows, columns, CH
        )


def conv(src, row, rows, columns, weight, bias):
    lhs = jnp.concatenate(
        [src[pl.ds(row + a, rows)].reshape(rows * columns, 3 * CH) for a in range(3)], axis=1
    )
    return jnp.dot(lhs, weight, preferred_element_type=F32) + bias


def inside(value, first, columns, height):
    cells = value.shape[0]
    row = first + lax.broadcasted_iota(jnp.int32, (cells, 1), 0) // columns
    return jnp.where((row >= 0) & (row < height), value, 0.0)


def chunks(rows, step):
    return [(r, min(step, rows - r)) for r in range(0, rows, step)]


def project(cells, weight, bias):
    return (jnp.dot(cells, weight, preferred_element_type=F32) + bias).astype(BF)


def lift(table, cells):
    return jnp.dot(table, cells, preferred_element_type=F32).astype(BF)


def load(sems, *pairs):
    copies = [pltpu.make_async_copy(src, dst, sems.at[k]) for k, (src, dst) in enumerate(pairs)]
    for copy in copies:
        copy.start()
    return copies


def pair_up(hop, devices, parts):
    inner = [i ^ hop for i in range(devices)]
    outer = [((i - hop) ^ hop) + hop for i in range(devices)]
    return [
        [
            (p * devices + i, p * devices + j if 0 <= j < devices else (p ^ 1) * devices + i)
            for p in range(parts)
            for i, j in enumerate(ends)
        ]
        for ends in (inner, outer)
    ]


def first_half(hop):
    return (lax.axis_index("rows") // hop) % 2 == 0


def sides(inner, outer, hop):
    lower = first_half(hop)
    return jnp.where(lower, outer, inner), jnp.where(lower, inner, outer)


def edge_rows(fine, flag):
    start = jnp.where(first_half(1) == flag, 384, 0)
    return fine.at[pl.ds(pl.multiple_of(start, 128), 640)]


def pack_kernel(third, second, fine, pack, outer, far, sems):
    copies = load(
        sems,
        (edge_rows(fine, False), outer),
        (second, pack.at[pl.ds(64, 256)]),
        (third, pack.at[pl.ds(0, 64)]),
        (third, far),
    )
    for copy in copies:
        copy.wait()


def middle_kernel(fine, w, conv_bias, h_mid, lat_mid, inner, x1):
    inner[...] = edge_rows(fine, True)[...]
    c1 = 128
    for r in (0, 4):
        store_taps(x1, r, jnp.maximum(fine[r * c1 : (r + 4) * c1].astype(F32), 0.0), c1)
    for r, n in chunks(6, 3):
        hid = jnp.maximum(conv(x1, r, n, c1, w[6], conv_bias[6:7]), 0.0)
        store_taps(h_mid, r, hid, c1)
    lat_mid[...] = conv(h_mid, 0, 4, c1, w[7], conv_bias[7:8]) + fine[2 * c1 : 6 * c1].astype(F32)


def clamped(above, own, below, columns):
    position = lax.axis_index("rows")
    ends = lax.axis_size("rows") - 1
    last = above.shape[0] - columns
    above_row = jnp.where(position == 0, own[0:columns], above[last:])
    below_row = jnp.where(position == ends, own[own.shape[0] - columns :], below[0:columns])
    return jnp.concatenate([above[0:last], above_row, own, below_row, below[columns:]], axis=0)


def coarse_kernel(
    inner2, outer2, inner1, outer1, second, third, w, conv_bias, out_weight, out_bias, table3,
    u_inner, u_outer, x3, h3, x2, h2, p2nd, merged, kept,
):
    position = lax.axis_index("rows")
    ends = lax.axis_size("rows") - 1
    c3, c2 = 32, 64
    base3, base2 = 2 * position, 4 * position
    high3, high2 = 2 * (ends + 1), 4 * (ends + 1)
    m1, p1 = sides(inner1[...], outer1[...], 1)
    m2, p2 = sides(inner2[...], outer2[...], 2)

    raw3 = jnp.concatenate([m2, m1[0:64], third[...], p1[0:64], p2], axis=0).astype(F32)
    store_taps(x3, 0, inside(jnp.maximum(raw3, 0.0), base3 - 4, c3, high3), c3)
    for row, part in ((0, m1[64:320]), (4, second[...]), (8, p1[64:320])):
        value = jnp.maximum(part.astype(F32), 0.0)
        store_taps(x2, row, inside(value, base2 + row - 4, c2, high2), c2)

    hid = jnp.maximum(conv(x3, 0, 8, c3, w[0], conv_bias[0:1]), 0.0)
    store_taps(h3, 0, inside(hid, base3 - 3, c3, high3), c3)
    for r, n in chunks(10, 5):
        hid = jnp.maximum(conv(x2, r, n, c2, w[2], conv_bias[2:3]), 0.0)
        store_taps(h2, r, inside(hid, base2 - 3 + r, c2, high2), c2)
    path = conv(h3, 0, 6, c3, w[1], conv_bias[1:2]) + raw3[64:256]
    u = project(path.astype(BF), out_weight[0], out_bias[0:1])
    u = clamped(u[0:64], u[64:128], u[128:192], c3)
    for j in range(5):
        two = lift(table3[...], u[j * c3 : (j + 2) * c3])
        if j > 0:
            p2nd[2 * j - 1] = two[0:c2]
        if j < 4:
            p2nd[2 * j] = two[c2 : 2 * c2]

    raw2 = jnp.concatenate([m1[192:320], second[...], p1[64:192]], axis=0)
    for r, n in chunks(8, 2):
        lateral = conv(h2, r, n, c2, w[3], conv_bias[3:4])
        lateral = lateral + raw2[r * c2 : (r + n) * c2].astype(F32)
        joined = (lateral + p2nd[pl.ds(r, n)].reshape(n * c2, CH).astype(F32)).astype(BF)
        merged[pl.ds(r, n)] = joined.reshape(n, c2, CH)
        value = jnp.maximum(joined.astype(F32), 0.0)
        store_taps(x2, r, inside(value, base2 - 2 + r, c2, high2), c2)
    for r, n in chunks(6, 2):
        hid = jnp.maximum(conv(x2, r, n, c2, w[4], conv_bias[4:5]), 0.0)
        store_taps(h2, r, inside(hid, base2 - 1 + r, c2, high2), c2)
    for r, n in chunks(4, 2):
        refined = conv(h2, r, n, c2, w[5], conv_bias[5:6])
        refined = refined + merged[r + 2 : r + 2 + n].reshape(n * c2, CH).astype(F32)
        kept[r * c2 : (r + n) * c2] = project(
            refined.astype(BF), out_weight[1], out_bias[1:2]
        )
    lower = first_half(1)
    start = [pl.multiple_of(jnp.where(lower == flag, 128, 0), 128) for flag in (True, False)]
    u_inner[...] = kept[pl.ds(start[0], 128)]
    u_outer[...] = kept[pl.ds(start[1], 128)]


def lateral_kernel(
    inner, outer, fine, w, conv_bias, h_mid, lat_top, lat_end, x_top, x_end, h_top, h_end,
):
    position = lax.axis_index("rows")
    ends = lax.axis_size("rows") - 1
    c1 = 128
    base, height = 8 * position, 8 * (ends + 1)
    mf, pf = sides(inner[...], outer[...], 1)
    raw_top = jnp.concatenate([mf, fine[0:256]], axis=0)
    raw_end = jnp.concatenate([fine[768:1024], pf], axis=0)
    h_top[5:7] = h_mid[0:2]
    h_end[0:2] = h_mid[4:6]
    for x, raw, first in ((x_top, raw_top, -5), (x_end, raw_end, 6)):
        for r, n in chunks(7, 4):
            value = jnp.maximum(raw[r * c1 : (r + n) * c1].astype(F32), 0.0)
            store_taps(x, r, inside(value, base + first + r, c1, height), c1)
    for x, h, first, at in ((x_top, h_top, -4, 0), (x_end, h_end, 7, 2)):
        for r, n in chunks(5, 3):
            hid = jnp.maximum(conv(x, r, n, c1, w[6], conv_bias[6:7]), 0.0)
            store_taps(h, at + r, inside(hid, base + first + r, c1, height), c1)
    for h, raw, skip, lateral in ((h_top, raw_top, 2, lat_top), (h_end, raw_end, 0, lat_end)):
        part = raw[skip * c1 : (skip + 5) * c1].astype(F32)
        lateral[...] = conv(h, 0, 5, c1, w[7], conv_bias[7:8]) + part


def fine_kernel(
    lat_top, lat_mid, lat_end, u_inner, u_outer, inner_u, outer_u, w, conv_bias, out_weight,
    out_bias, table2, table1, out, p1st, x1, hb, merged, u1, staged, sems,
):
    position = lax.axis_index("rows")
    ends = lax.axis_size("rows") - 1
    c2, c1 = 64, 128
    base, height = 8 * position, 8 * (ends + 1)
    mu, pu = sides(inner_u[...], outer_u[...], 1)
    above, below = sides(u_inner[...], u_outer[...], 1)
    u = clamped(mu, jnp.concatenate([above, below], axis=0), pu, c2)
    def merge(lateral, r, n, pairs):
        for j in pairs:
            two = lift(table2[...], u[j * c2 : (j + 2) * c2])
            p1st[2 * j : 2 * j + 2] = two.reshape(2, c1, CH)
        joined = (lateral[...] + p1st[pl.ds(r, n)].reshape(n * c1, CH).astype(F32)).astype(BF)
        merged[pl.ds(r, n)] = joined.reshape(n, c1, CH)
        value = jnp.maximum(joined.astype(F32), 0.0)
        store_taps(x1, r, inside(value, base - 3 + r, c1, height), c1)

    def hidden(r, n):
        hid = jnp.maximum(conv(x1, r, n, c1, w[8], conv_bias[8:9]), 0.0)
        store_taps(hb, r, inside(hid, base - 2 + r, c1, height), c1)

    merge(lat_top, 0, 5, range(0, 3))
    merge(lat_mid, 5, 4, range(3, 5))
    merge(lat_end, 9, 5, range(5, 7))
    hidden(0, 4)
    hidden(4, 4)
    hidden(8, 4)
    copies = []
    for r, n in chunks(10, 5):
        refined = conv(hb, r, n, c1, w[9], conv_bias[9:10])
        refined = refined + merged[pl.ds(r + 2, n)].reshape(n * c1, CH).astype(F32)
        u1[r * c1 : (r + n) * c1] = project(refined.astype(BF), out_weight[2], out_bias[2:3])
        edge, row, flag = (0, c1, 0) if r == 0 else (9 * c1, 8 * c1, ends)
        u1[edge : edge + c1] = jnp.where(
            position == flag, u1[row : row + c1], u1[edge : edge + c1]
        )
        for j in range(0, 4) if r == 0 else range(4, 9):
            first, count = max(2 * j - 1, 0), 2 if 0 < j < 8 else 1
            half = slice(2 * c1 if j == 0 else 0, 2 * c1 if j == 8 else 4 * c1)
            rows = lift(table1[half], u1[j * c1 : (j + 2) * c1])
            staged[pl.ds(first, count)] = rows.reshape(count, 2 * c1, CH)
            copies.append(
                pltpu.make_async_copy(
                    staged.at[pl.ds(first, count)], out.at[pl.ds(first, count)], sems.at[j]
                )
            )
            copies[-1].start()
    for copy in copies:
        copy.wait()


VM = pl.BlockSpec(memory_space=pltpu.VMEM)
ANY = pl.BlockSpec(memory_space=pltpu.HBM)


def call(kernel, in_vmem, in_hbm, outs, out_spec, scratch, sems, flops):
    return pl.pallas_call(
        kernel,
        out_shape=[jax.ShapeDtypeStruct(shape, kind) for shape, kind in outs],
        in_specs=[VM] * len(in_vmem) + [ANY] * len(in_hbm),
        out_specs=[out_spec] * len(outs),
        scratch_shapes=[pltpu.VMEM(shape, kind) for shape, kind in scratch]
        + [pltpu.SemaphoreType.DMA((sems,))] * (sems > 0),
        compiler_params=pltpu.CompilerParams(vmem_limit_bytes=VMEM_LIMIT),
        cost_estimate=pl.CostEstimate(flops=flops, bytes_accessed=1_000_000, transcendentals=0),
    )(*in_vmem, *(pltpu.with_memory_space_constraint(x, pltpu.HBM) for x in in_hbm))


def local(feat_fine, feat_second, feat_third, conv_weight, conv_bias, out_weight, out_bias):
    devices = lax.axis_size("rows")

    def exchange(value_in, value_out, hop):
        values = (value_in, value_out)
        pairs = pair_up(hop, devices, lax.axis_size("img"))
        return [lax.ppermute(v, ("img", "rows"), p) for v, p in zip(values, pairs)]

    third = feat_third.reshape(64, CH)
    second = feat_second.reshape(256, CH)
    fine = feat_fine.reshape(1024, CH)
    weight = conv_weight.reshape(10, TAPS, CH)
    pack, fine_out, third_out = call(
        pack_kernel,
        (),
        (third, second, fine),
        [((320, CH), BF), ((640, CH), BF), ((64, CH), BF)],
        VM,
        [],
        4,
        PACK_COST,
    )
    far = exchange(third_out, third_out, 2)
    near = exchange(pack, pack, 1)
    h_mid, lat_mid, fine_in = call(
        middle_kernel,
        (fine, weight, conv_bias),
        (),
        [((6, 128, 3 * CH), BF), ((512, CH), F32), ((640, CH), BF)],
        VM,
        [((8, 128, 3 * CH), BF)],
        0,
        FETCH_COST,
    )
    halo = exchange(fine_in, fine_out, 1)
    u2 = call(
        coarse_kernel,
        (*far, *near, second, third, weight, conv_bias, out_weight, out_bias, pair_table(32)),
        (),
        [((128, CH), BF)] * 2,
        VM,
        [
            ((10, 32, 3 * CH), BF),
            ((8, 32, 3 * CH), BF),
            ((12, 64, 3 * CH), BF),
            ((10, 64, 3 * CH), BF),
            ((8, 64, CH), BF),
            ((8, 64, CH), BF),
            ((256, CH), BF),
        ],
        0,
        4_000_000_000,
    )
    got = exchange(*u2, 1)
    lat_top, lat_end = call(
        lateral_kernel,
        (*halo, fine, weight, conv_bias, h_mid),
        (),
        [((640, CH), F32)] * 2,
        VM,
        [((7, 128, 3 * CH), BF)] * 4,
        0,
        4_000_000_000,
    )
    (out,) = call(
        fine_kernel,
        (
            lat_top, lat_mid, lat_end, *u2, *got, weight, conv_bias, out_weight, out_bias,
            pair_table(64), pair_table(128),
        ),
        (),
        [((16, 256, CH), BF)],
        ANY,
        [
            ((14, 128, CH), BF),
            ((14, 128, 3 * CH), BF),
            ((12, 128, 3 * CH), BF),
            ((14, 128, CH), BF),
            ((1280, CH), BF),
            ((16, 256, CH), BF),
        ],
        9,
        4_000_000_000,
    )
    return out


def solution(mesh):
    rows = P(("img", "rows"), None, None)
    return jax.shard_map(
        local,
        mesh=mesh,
        in_specs=(rows, rows, rows, P(), P(), P(), P()),
        out_specs=rows,
        check_vma=False,
    )
```
